32 devices in a mesh: pole: 2 (over x), row: 16 (over z, y, core).
Axes of the slice: x: 2, y: 2, z: 4, core: 2. Of those that a mesh axis runs over, the one named last changes fastest.
Arguments:
- root_inverse: float32 [4096, 2048], P(('pole', 'row')), parts along dimension 0, may hold values from -6 to 6
- panels: float32 [32, 1024, 512], P(('pole', 'row')), parts along dimension 0, may hold values from -0.1875 to 0.1875
- diag_blocks: float32 [32, 512, 512], P(('pole', 'row')), parts along dimension 0, may hold values from -3 to 3
- structure: int32 [16, 1024], replicated, may hold values from 0 to 2047, as said below
- live: int32 [16], replicated, may hold values from 256 to 1024, as said below
Outputs:
- block_rows: float32 [4096, 16, 512], P(('pole', 'row')), parts along dimension 0
- child_inverse: float32 [32, 512, 512], P(('pole', 'row')), parts along dimension 0
The draws below stay inside these ranges and needn't reach their ends.
There are 2 independent parts, one for each index of `pole`. The reference program is written for one: setup_inputs(seed, part) draws one part's arguments, and reference() takes and returns one part's arrays. A program takes and returns all parts, laid end to end along the dimension named above; an argument that names none is the same for every part. Nothing has to cross between parts.
Inputs may be any that keep to these rules, and one draw needn't show every extreme that they name: `structure`: row j holds live[j] distinct root rows in increasing order, then zeros. `live`: the largest is 1024 in every draw.
All inputs are finite; a program needn't handle non-finite values.
Results may differ from the reference program's by a relative error of at most 0.0003.
Values sent between devices are 32-bit elements; how exact they have to be, the bound alone decides.
No kernel may reach another device: no remote copies, remote signals or barrier semaphores. Data moves between devices by JAX's collectives and lax.ppermute only.
A program may use at most 128 MiB of HBM per device.

```python
import jax
import jax.numpy as jnp
from jax import lax

RW = 2048
W = 512
P_SIZE = 1024
CHILD = 16


def child_counts(key):
    key = jax.random.fold_in(key, 7)
    counts = jax.random.randint(key, (CHILD,), P_SIZE // 4, P_SIZE + 1)
    fullest = jax.random.randint(jax.random.fold_in(key, 1), (), 0, CHILD)
    return counts.at[fullest].set(P_SIZE).astype(jnp.int32)


def draw_live(key, part):
    return child_counts(key)


def draw_structure(key, part):
    counts = child_counts(key)
    key = jax.random.fold_in(key, 3)
    keys = jax.random.split(key, CHILD)
    chosen = jax.vmap(lambda k: jax.random.permutation(k, RW)[:P_SIZE])(keys).astype(jnp.int32)
    positions = jnp.arange(P_SIZE, dtype=jnp.int32)[None, :]
    chosen = jnp.where(positions < counts[:, None], chosen, RW)
    chosen = jnp.sort(chosen, axis=1)
    return jnp.where(chosen == RW, 0, chosen).astype(jnp.int32)


def block_levels(key, extent, pieces, least, largest):
    factor_of = 1.0
    for axis_at, parts in pieces:
        draws = jax.random.uniform(jax.random.fold_in(jax.random.fold_in(key, 6), axis_at), (parts,), jnp.float32, least / len(pieces), largest / len(pieces))
        factor_of = factor_of * jnp.repeat(jnp.exp(draws), extent[axis_at] // parts).reshape((-1,) + (1,) * (len(extent) - 1 - axis_at))
    return factor_of


def bell_draw(stream_key, shape, spread, bound, shards=(), kind=jnp.bfloat16):
    drawn = jax.random.normal(stream_key, shape, jnp.float32) * spread
    if len(shards) > 0:
        drawn = block_levels(stream_key, shape, shards, -0.22, 0.18) * drawn
    return jnp.clip(drawn, min=-bound, max=bound).astype(kind)


def setup_inputs(seed: int = 0, part: int = 0) -> dict:
    splits = jax.random.split(jax.random.key(seed), 6)
    own_keys = jax.random.split(jax.random.fold_in(splits[5], part), 6)
    return {
        "root_inverse": bell_draw(own_keys[0], (RW, RW), 1.0, 6.0, ((0, 16),), jnp.float32),
        "panels": bell_draw(own_keys[1], (CHILD, P_SIZE, W), P_SIZE ** -0.5, 0.1875, ((0, 16),), jnp.float32),
        "diag_blocks": bell_draw(own_keys[2], (CHILD, W, W), 0.5, 3.0, ((0, 16),), jnp.float32),
        "structure": draw_structure(jax.random.fold_in(splits[5], 71), part),
        "live": draw_live(jax.random.fold_in(splits[5], 71), part),
    }


def reference(root_inverse, panels, diag_blocks, structure, live):
    def child_step(args):
        rows, count, panel, diag = args
        positions = jnp.arange(rows.shape[0], dtype=jnp.int32)
        mask = (positions < count).astype(root_inverse.dtype)
        sub = jnp.take(jnp.take(root_inverse, rows, axis=0), rows, axis=1)
        masked = panel * mask[:, None]
        off = -jnp.dot(sub, masked, precision=lax.Precision.HIGHEST) * mask[:, None]
        inner = diag - jnp.dot(masked.T, off, precision=lax.Precision.HIGHEST)
        return off, inner

    offs, child_inverse = lax.map(child_step, (structure, live, panels, diag_blocks))
    owners = jnp.arange(structure.shape[0], dtype=jnp.int32)[:, None] + jnp.zeros_like(structure)
    block_rows = jnp.zeros((root_inverse.shape[0], structure.shape[0], panels.shape[2]), root_inverse.dtype)
    block_rows = block_rows.at[structure, owners].add(offs)
    return block_rows, child_inverse
```

```python
import functools

import jax
import jax.numpy as jnp
from jax import lax
from jax.experimental import pallas as pl
from jax.experimental.pallas import tpu as pltpu
from jax.sharding import PartitionSpec as P

F32 = jnp.float32
BF16 = jnp.bfloat16
PLANES = 4
PLANE = 4
LANES = 128
VMEM_BYTES = 48 * 1024 * 1024


def split(x):
    hi = x.astype(BF16)
    return hi, (x - hi.astype(F32)).astype(BF16)


def dot(a, b):
    return jnp.dot(a, b, preferred_element_type=F32)


def dot_t(a, b):
    return lax.dot_general(a, b, (((0,), (0,)), ((), ())), preferred_element_type=F32)


class Table:
    def __init__(self, children, blocks):
        self.children, self.blocks = children, blocks
        self.first = 0
        self.offset = children * blocks
        self.live = 2 * children * blocks
        self.me = self.live + children
        self.size = self.me + 1


def window(tab, t, s_ref, child, block, rows, padded):
    span = min(2 * rows, padded)
    begin = tab[t.first + child * t.blocks + block]
    at = pl.multiple_of(jnp.minimum((begin // rows) * rows, padded - span), rows)
    row_ids = lax.broadcasted_iota(jnp.int32, (rows, span), 0) + block * rows
    positions = lax.broadcasted_iota(jnp.int32, (rows, span), 1) + at
    hit = (row_ids == s_ref[child, :, pl.ds(at, span)]) & (positions < tab[t.live + child])
    return at, span, positions, hit


def slots(tab, t, s_ref, child, block, rows, padded):
    _, _, positions, hit = window(tab, t, s_ref, child, block, rows, padded)
    shift = tab[t.offset + child * t.blocks + block] - tab[t.first + child * t.blocks + block]
    return jnp.max(jnp.where(hit, positions + shift, -1), axis=1, keepdims=True)


def spread_kernel(t, flips, tab, s_ref, *refs):
    panels, (hi_ref, lo_ref) = refs[: len(flips)], refs[len(flips) :]
    total, width = hi_ref.shape[1:]
    padded = s_ref.shape[2]
    rows = total // t.blocks
    for c, flip in enumerate(flips):
        child = tab[t.me] ^ flip
        panel = panels[c]

        def step(block, carry):
            at, span, _, hit = window(tab, t, s_ref, child, block, rows, padded)
            hot = hit.astype(BF16)
            hi, lo = split(panel[0, pl.ds(at, span), :])
            to = pl.ds(pl.multiple_of(block * rows, rows), rows)
            hi_ref[c, to, :] = dot(hot, hi).astype(BF16)
            lo_ref[c, to, :] = dot(hot, lo).astype(BF16)
            return carry

        lax.fori_loop(0, t.blocks, step, 0)


def product_kernel(groups, *refs):
    count = sum(groups)
    blocks, (hi_ref, lo_ref, out_ref, x_ref) = refs[:count], refs[count:]
    rows = blocks[0].shape[0]
    m = rows * len(groups)

    @pl.when(pl.program_id(0) == 0)
    def _():
        at = 0
        for k, size in enumerate(groups):
            whole = blocks[at][...]
            for other in range(1, size):
                whole = whole + blocks[at + other][...]
            at += size
            hi, lo = split(whole)
            x_ref[pl.ds(k * rows, rows), :] = hi
            x_ref[pl.ds(m + k * rows, rows), :] = lo

    both = dot(x_ref[...], hi_ref[0])
    out_ref[0] = both[:m] + both[m:] + dot(x_ref[:m, :], lo_ref[0])


def pack_kernel(t, deltas, cap, tab, s_ref, first_ref, second_ref, *outs):
    rows = first_ref.shape[1] // len(deltas)
    padded = s_ref.shape[2]
    me = tab[t.me]
    slot_ids = lax.broadcasted_iota(jnp.int32, (rows, cap), 1)
    for k, delta in enumerate(deltas):
        block = delta(me, t.blocks)
        total = None
        for flip in range(PLANE):
            source = first_ref if flip < 2 else second_ref
            values = source[flip % 2, pl.ds(k * rows, rows), :]
            hi, lo = split(values)
            hot = (slots(tab, t, s_ref, me ^ flip, block, rows, padded) == slot_ids).astype(BF16)
            part = dot_t(hot, hi) + dot_t(hot, lo)
            total = part if total is None else total + part
        outs[k][...] = total


def own(me, blocks):
    return me


def below(me, blocks):
    return jnp.maximum(me - PLANE, 0)


def above(me, blocks):
    return jnp.minimum(me + PLANE, blocks - 1)


def across(me, blocks):
    return me ^ (2 * PLANE)


def mirror(me, blocks):
    return me ^ (3 * PLANE)


def expand_kernel(t, cap, tab, s_ref, *refs):
    messages, out_ref, lanes_ref = refs[:-2], refs[-2], refs[-1]
    total, width = out_ref.shape
    rows = total // t.children
    lanes = lanes_ref.shape[1]
    padded = s_ref.shape[2]
    me = tab[t.me]
    z = me // PLANE
    sources = (
        (z, z >= 0),
        (z - 1, z > 0),
        (z + 1, z < PLANES - 1),
        (z ^ 2, z >= 0),
        (z ^ 3, (z == 0) | (z == PLANES - 1)),
    )
    slot_ids = lax.broadcasted_iota(jnp.int32, (rows, cap), 1)
    for message, (plane, there) in zip(messages, sources):

        @pl.when(there)
        def _():
            hi, lo = split(message[...])
            for c in range(PLANE):
                child = plane * PLANE + c
                hot = (slots(tab, t, s_ref, child, me, rows, padded) == slot_ids).astype(BF16)
                value = -(dot(hot, hi) + dot(hot, lo))
                for k in range(width // lanes):
                    to = pl.ds(k * total + child, rows, stride=t.children)
                    lanes_ref[to, :] = value[:, k * lanes : (k + 1) * lanes]
    for k in range(width // lanes):
        out_ref[:, k * lanes : (k + 1) * lanes] = lanes_ref[k * total : (k + 1) * total, :]


def inner_kernel(where, tab, *refs):
    count = len(where)
    products, factors_hi, factors_lo, out_ref = (
        refs[:count],
        refs[count : 2 * count],
        refs[2 * count : 3 * count],
        refs[-1],
    )
    total = None
    for g, bh, bl in zip(products, factors_hi, factors_lo):
        hi, lo = split(g[0])
        part = dot_t(bh[0], hi) + dot_t(bh[0], lo) + dot_t(bl[0], hi)
        total = part if total is None else total + part
    out_ref[0] = total


def vmem():
    return pl.BlockSpec(memory_space=pltpu.VMEM)


def smem():
    return pl.BlockSpec(memory_space=pltpu.SMEM)


def params():
    return pltpu.CompilerParams(vmem_limit_bytes=VMEM_BYTES)


def cost(flops, bytes_accessed):
    return pl.CostEstimate(flops=int(flops), bytes_accessed=int(bytes_accessed), transcendentals=0)


def planes_body(cap, table, root_inverse, panels, diag_blocks, structure3):
    rows, total = root_inverse.shape
    children = structure3.shape[0]
    blocks = total // rows
    width = panels.shape[2]
    padded = panels.shape[1]
    t = Table(children, blocks)
    at = range(blocks)

    def permute(x, move):
        pairs = [(r, move(r)) for r in at if 0 <= move(r) < blocks]
        return lax.ppermute(x, "row", pairs)

    def along(x, planes, step):
        return lax.ppermute(
            x, "row", [(p * PLANE + b, (p + step) * PLANE + b) for p in planes for b in range(PLANE)]
        )

    panel_1 = permute(panels, lambda r: r ^ 1)
    panel_2 = permute(panels, lambda r: r ^ 2)
    from_below = along(root_inverse, range(PLANES - 1), 1)
    from_above = along(root_inverse, range(1, PLANES), -1)
    panel_3 = permute(panel_2, lambda r: r ^ 1)
    below_2 = along(from_below, range(1, PLANES - 1), 1)
    above_2 = along(from_above, range(1, PLANES - 1), -1)
    below_3 = along(below_2, range(2, PLANES - 1), 1)
    above_3 = along(above_2, range(1, 2), -1)

    def spread(flips, *given):
        shape = jax.ShapeDtypeStruct((len(flips), total, width), BF16)
        return pl.pallas_call(
            functools.partial(spread_kernel, t, flips),
            out_shape=(shape, shape),
            in_specs=[smem(), vmem()] + [vmem()] * len(given),
            out_specs=(vmem(), vmem()),
            compiler_params=params(),
            cost_estimate=cost(8 * len(flips) * total * rows * 2 * width, 6 * len(flips) * total * width),
            name="spread",
        )(table, structure3, *given)

    def product(groups, factors, *given):
        hi, lo = factors
        m = rows * len(groups)
        return pl.pallas_call(
            functools.partial(product_kernel, groups),
            grid=(2,),
            out_shape=jax.ShapeDtypeStruct((2, m, width), F32),
            in_specs=[pl.BlockSpec((rows, total), lambda c: (0, 0))] * len(given)
            + [pl.BlockSpec((1, total, width), lambda c: (c, 0, 0))] * 2,
            out_specs=pl.BlockSpec((1, m, width), lambda c: (c, 0, 0)),
            scratch_shapes=[pltpu.VMEM((2 * m, total), BF16)],
            compiler_params=params(),
            cost_estimate=cost(12 * m * total * width, 4 * len(given) * rows * total + 8 * total * width),
            name="product",
        )(*given, hi, lo)

    def pack(deltas, first, second):
        out = jax.ShapeDtypeStruct((cap, width), F32)
        return pl.pallas_call(
            functools.partial(pack_kernel, t, deltas, cap),
            out_shape=[out] * len(deltas),
            in_specs=[smem(), vmem(), vmem(), vmem()],
            out_specs=[vmem()] * len(deltas),
            compiler_params=params(),
            cost_estimate=cost(16 * len(deltas) * cap * rows * width, 4 * len(deltas) * (cap + 4 * rows) * width),
            name="pack",
        )(table, structure3, first, second)

    factors_a = spread((0, 1), panels, panel_1)
    near_a = product((1, 1, 1), factors_a, root_inverse, from_below, from_above)
    far_a = product((2,), factors_a, below_2, above_2)
    factors_b = spread((2, 3), panel_2, panel_3)
    near_b = product((1, 1, 1), factors_b, root_inverse, from_below, from_above)
    kept, down, up = pack((own, below, above), near_a, near_b)
    got_below = along(up, range(PLANES - 1), 1)
    got_above = along(down, range(1, PLANES), -1)
    far_b = product((2,), factors_b, below_2, above_2)
    (twice,) = pack((across,), far_a, far_b)
    got_across = permute(twice, lambda r: r ^ (2 * PLANE))
    last_a = product((2,), factors_a, below_3, above_3)
    last_b = product((2,), factors_b, below_3, above_3)
    (thrice,) = pack((mirror,), last_a, last_b)
    ends = (0, PLANES - 1)
    got_mirror = lax.ppermute(
        thrice, "row", [(p * PLANE + b, (PLANES - 1 - p) * PLANE + b) for p in ends for b in range(PLANE)]
    )

    where = (own, below, above, across, mirror)

    def inner(factors, near, far, last):
        def source(k):
            return pl.BlockSpec((1, rows, width), lambda c, tab: (c, k, 0))

        def factor(delta):
            return pl.BlockSpec((1, rows, width), lambda c, tab: (c, delta(tab[t.me], blocks), 0))

        return pl.pallas_call(
            functools.partial(inner_kernel, where),
            out_shape=jax.ShapeDtypeStruct((2, width, width), F32),
            grid_spec=pltpu.PrefetchScalarGridSpec(
                num_scalar_prefetch=1,
                grid=(2,),
                in_specs=[source(0), source(1), source(2), source(0), source(0)]
                + [factor(delta) for delta in where] * 2,
                out_specs=pl.BlockSpec((1, width, width), lambda c, tab: (c, 0, 0)),
            ),
            compiler_params=params(),
            cost_estimate=cost(12 * 5 * rows * width * width, 40 * rows * width + 8 * width * width),
            name="inner",
        )(table, near, near, near, far, last, *([factors[0]] * 5), *([factors[1]] * 5))

    inner_a = inner(factors_a, near_a, far_a, last_a)
    inner_b = inner(factors_b, near_b, far_b, last_b)
    sibling = permute(jnp.stack([inner_a[1], inner_b[1]]), lambda r: r ^ 1)
    other = permute(inner_b[0] + sibling[1], lambda r: r ^ 2)
    child_inverse = diag_blocks + (inner_a[0] + sibling[0] + other)[None]

    messages = (kept, got_below, got_above, got_across, got_mirror)
    block_rows = pl.pallas_call(
        functools.partial(expand_kernel, t, cap),
        out_shape=jax.ShapeDtypeStruct((rows * children, width), F32),
        in_specs=[smem(), vmem()] + [vmem()] * len(messages),
        out_specs=vmem(),
        scratch_shapes=[pltpu.VMEM((rows * children * (width // LANES), LANES), F32)],
        compiler_params=params(),
        cost_estimate=cost(4 * rows * children * cap * width, 4 * (rows * children + 5 * cap) * width),
        name="expand",
    )(table, structure3, *messages)
    return block_rows.reshape(rows, children, width), child_inverse


def planes(root_inverse, panels, diag_blocks, structure, live):
    rows, total = root_inverse.shape
    children, padded = structure.shape
    blocks = total // rows
    positions = jnp.arange(padded, dtype=jnp.int32)
    block_of = jnp.where(positions[None, :] < live[:, None], structure // rows, blocks)
    edges = jnp.arange(blocks + 1, dtype=jnp.int32)
    first = jnp.sum((block_of[:, None, :] < edges[None, :, None]).astype(jnp.int32), axis=2)
    counts = (first[:, 1:] - first[:, :-1]).reshape(PLANES, PLANE, blocks)
    offsets = [jnp.zeros_like(counts[:, 0])]
    for c in range(PLANE):
        offsets.append(offsets[-1] + counts[:, c])
    largest = jnp.max(offsets[-1])
    offset = jnp.stack(offsets[:-1], axis=1).reshape(children, blocks)
    table = jnp.concatenate(
        [
            first[:, :-1].reshape(-1),
            offset.reshape(-1),
            live,
            lax.axis_index("row").astype(jnp.int32)[None],
        ]
    )
    caps = (PLANE * rows // 2, PLANE * rows)
    branch = sum((largest > cap).astype(jnp.int32) for cap in caps[:-1])
    return lax.switch(
        branch,
        [functools.partial(planes_body, cap) for cap in caps],
        table,
        root_inverse,
        panels,
        diag_blocks,
        structure.reshape(children, 1, padded),
    )


def body(root_inverse, panels, diag_blocks, structure, live):
    me = lax.axis_index("row")
    rows_here = root_inverse.shape[0]
    padded = structure.shape[1]
    width = panels.shape[2]
    total_rows = rows_here * lax.axis_size("row")
    mine = lax.dynamic_index_in_dim(structure, me, 0, keepdims=False)
    count = lax.dynamic_index_in_dim(live, me, 0, keepdims=False)
    columns = jnp.take(lax.all_gather(root_inverse, "row", axis=0, tiled=True), mine, axis=1)
    sub = jnp.take(columns, mine, axis=0)
    positions = jnp.arange(padded, dtype=jnp.int32)
    mask = (positions < count).astype(jnp.float32)
    masked = panels[0] * mask[:, None]
    off = -jnp.dot(sub, masked, precision=lax.Precision.HIGHEST) * mask[:, None]
    inner = diag_blocks[0] - jnp.dot(masked.T, off, precision=lax.Precision.HIGHEST)
    spread = jnp.zeros((total_rows, width), jnp.float32).at[mine].add(off)
    block_rows = lax.all_to_all(
        spread.reshape(total_rows, 1, width), "row", split_axis=0, concat_axis=1, tiled=True
    )
    return (block_rows, inner[None])


def solution(mesh):
    placed = (
        P(("pole", "row"), None),
        P(("pole", "row"), None, None),
        P(("pole", "row"), None, None),
        P(),
        P(),
    )
    return jax.shard_map(
        planes if mesh.shape["row"] == PLANES * PLANE else body,
        mesh=mesh,
        in_specs=placed,
        out_specs=(P(("pole", "row"), None, None), P(("pole", "row"), None, None)),
        check_vma=False,
    )
```

```python
import functools

import jax
import jax.numpy as jnp
from jax import lax
from jax.experimental import pallas as pl
from jax.experimental.pallas import tpu as pltpu
from jax.sharding import PartitionSpec as P

F32 = jnp.float32
BF16 = jnp.bfloat16
PLANES = 4
PLANE = 4
LANES = 128
SCALE = 16
VMEM_BYTES = 36 * 1024 * 1024
LARGE_BYTES = 58 * 1024 * 1024


def split(x):
    hi = x.astype(BF16)
    return hi, (x - hi.astype(F32)).astype(BF16)


def dot(a, b):
    return jnp.dot(a, b, preferred_element_type=F32)


def dot_t(a, b):
    return lax.dot_general(a, b, (((0,), (0,)), ((), ())), preferred_element_type=F32)


class Table:
    def __init__(self, children, blocks):
        self.children, self.blocks = children, blocks
        self.first = 0
        self.offset = children * blocks
        self.live = 2 * children * blocks
        self.me = self.live + children
        self.over = self.me + 1


def window(tab, t, s_ref, child, block, rows, padded):
    span = min(2 * rows, padded)
    begin = tab[t.first + child * t.blocks + block]
    at = pl.multiple_of(jnp.minimum((begin // rows) * rows, padded - span), rows)
    row_ids = lax.broadcasted_iota(jnp.int32, (rows, span), 0) + block * rows
    positions = lax.broadcasted_iota(jnp.int32, (rows, span), 1) + at
    hit = (row_ids == s_ref[child, :, pl.ds(at, span)]) & (positions < tab[t.live + child])
    return at, span, positions, hit


def slots(tab, t, s_ref, child, block, rows, padded):
    _, _, positions, hit = window(tab, t, s_ref, child, block, rows, padded)
    shift = tab[t.offset + child * t.blocks + block] - tab[t.first + child * t.blocks + block]
    return jnp.max(jnp.where(hit, positions + shift, -1), axis=1, keepdims=True)


def spread_block(t, tab, s_ref, child, block, rows, panel, hi_ref, lo_ref, to):
    at, span, _, hit = window(tab, t, s_ref, child, block, rows, s_ref.shape[2])
    hot = hit.astype(BF16)
    hi, lo = split(panel[0, pl.ds(at, span), :])
    hi_ref[0, to, :] = dot(hot, hi).astype(BF16)
    lo_ref[0, to, :] = dot(hot, lo).astype(BF16)


def spread_kernel(t, flips, unroll, tab, s_ref, *refs):
    panels, (hi_ref, lo_ref) = refs[: len(flips)], refs[len(flips) :]
    rows = hi_ref.shape[1] // unroll
    for c, flip in enumerate(flips):

        @pl.when(pl.program_id(0) == c)
        def _():
            child = tab[t.me] ^ flip
            for u in range(unroll):
                block = pl.program_id(1) * unroll + u
                to = slice(u * rows, (u + 1) * rows)
                spread_block(t, tab, s_ref, child, block, rows, panels[c], hi_ref, lo_ref, to)


def product_kernel(t, flips, here, there, summed, spreads, deltas, cap, prior, tab, s_ref, *refs):
    count = len(here)
    priors, blocks, refs = refs[:prior], refs[prior : prior + count], refs[prior + count :]
    if spreads:
        panels, refs = refs[:2], refs[2:]
    if there:
        rest_ref, refs = refs[0], refs[1:]
    hi_ref, lo_ref, out_ref, refs = refs[0], refs[1], refs[2], refs[3:]
    if summed:
        kept_ref, sent_ref, refs = refs[0], refs[1], refs[2:]
    messages, x_ref = refs[:-1], refs[-1]
    rows = blocks[0].shape[0]
    m = rows * count
    padded = s_ref.shape[2]
    me = tab[t.me]
    step = pl.program_id(0)

    @pl.when(step == 0)
    def _():
        for k in range(count):
            hi, lo = split(blocks[k][...])
            x_ref[pl.ds(k * rows, rows), :] = hi
            x_ref[pl.ds(m + k * rows, rows), :] = lo

    if spreads:
        for c, flip in enumerate(flips):

            @pl.when(step == c)
            def _(panel=panels[c], flip=flip):
                for block in range(t.blocks):
                    to = slice(block * rows, (block + 1) * rows)
                    spread_block(t, tab, s_ref, me ^ flip, block, rows, panel, hi_ref, lo_ref, to)

    both = dot(x_ref[...], hi_ref[0])
    product = both[:m] + both[m:] + dot(x_ref[:m, :], lo_ref[0])
    out_ref[0] = product
    child = me ^ jnp.where(step == 0, flips[0], flips[1])
    slot_ids = lax.broadcasted_iota(jnp.int32, (rows, cap), 1)
    for n, (message, (k, delta)) in enumerate(zip(messages, deltas)):
        hot = slots(tab, t, s_ref, child, delta(me, t.blocks), rows, padded) == slot_ids
        hi, lo = split(product[k * rows : (k + 1) * rows])
        part = dot_t(hot.astype(BF16), hi) + dot_t(hot.astype(BF16), lo)

        @pl.when(step == 0)
        def _(n=n, message=message, part=part):
            message[...] = part + priors[n][...] if prior else part

        @pl.when(step != 0)
        def _(message=message, part=part):
            message[...] += part

    if summed:
        values = jnp.concatenate([product, rest_ref[0]], axis=0) if there else product
        at = [pl.multiple_of(delta(me, t.blocks) * rows, rows) for delta in here + there]
        bh = jnp.concatenate([hi_ref[0, pl.ds(k, rows), :] for k in at], axis=0)
        bl = jnp.concatenate([lo_ref[0, pl.ds(k, rows), :] for k in at], axis=0)
        hi, lo = split(values)
        inner = dot_t(bh, hi) + dot_t(bh, lo) + dot_t(bl, hi)

        @pl.when(step == 0)
        def _():
            kept_ref[...] = inner

        @pl.when(step != 0)
        def _():
            sent_ref[...] = inner


def last_kernel(t, cap, tab, s_ref, third_ref, hi_a, lo_a, hi_b, lo_b, out_ref, message, x_ref):
    rows = third_ref.shape[0]
    padded = s_ref.shape[2]
    me = tab[t.me]
    step = pl.program_id(0)

    @pl.when(step == 0)
    def _():
        hi, lo = split(third_ref[...])
        x_ref[:rows, :] = hi
        x_ref[rows:, :] = lo

    slot_ids = lax.broadcasted_iota(jnp.int32, (rows, cap), 1)
    for flip, (hi_ref, lo_ref) in enumerate(((hi_a, lo_a), (hi_a, lo_a), (hi_b, lo_b), (hi_b, lo_b))):

        @pl.when(step == flip)
        def _(flip=flip, hi_ref=hi_ref, lo_ref=lo_ref):
            both = dot(x_ref[...], hi_ref[0])
            product = both[:rows] + both[rows:] + dot(x_ref[:rows, :], lo_ref[0])
            out_ref[0] = product
            hot = slots(tab, t, s_ref, me ^ flip, mirror(me, t.blocks), rows, padded) == slot_ids
            hi, lo = split(product)
            part = dot_t(hot.astype(BF16), hi) + dot_t(hot.astype(BF16), lo)
            if flip == 0:
                message[...] = part
            else:
                message[...] += part


def finish_kernel(tab, diag_ref, kept_ref, sibling_ref, other_ref, *refs):
    products, (factors_hi, factors_lo, out_ref) = refs[:4], (refs[4:8], refs[8:12], refs[12])
    hi, lo = split(jnp.concatenate([g[0] for g in products], axis=0))
    bh = jnp.concatenate([b[0] for b in factors_hi], axis=0)
    bl = jnp.concatenate([b[0] for b in factors_lo], axis=0)
    added = dot_t(bh, hi) + dot_t(bh, lo) + dot_t(bl, hi)
    out_ref[0] = diag_ref[0] + (kept_ref[...] + sibling_ref[...] + other_ref[...] + added)


def own(me, blocks):
    return me


def below(me, blocks):
    return jnp.maximum(me - PLANE, 0)


def above(me, blocks):
    return jnp.minimum(me + PLANE, blocks - 1)


def across(me, blocks):
    return me ^ (2 * PLANE)


def mirror(me, blocks):
    return me ^ (3 * PLANE)


def store(lanes_ref, t, total, width, child, value, late=False):
    lanes = lanes_ref.shape[1]
    for k in range(width // lanes):
        to = pl.ds(k * total + child, total // t.children, stride=t.children)
        part = value[:, k * lanes : (k + 1) * lanes]
        lanes_ref[to, :] = lanes_ref[to, :] + part if late else part


def unpack(t, tab, s_ref, lanes_ref, total, message, plane, late=False):
    cap, width = message.shape
    rows = total // t.children
    slot_ids = lax.broadcasted_iota(jnp.int32, (rows, cap), 1) + (cap if late else 0)
    hi, lo = split(message[...])
    for c in range(PLANE):
        child = plane * PLANE + c
        hot = slots(tab, t, s_ref, child, tab[t.me], rows, s_ref.shape[2]) == slot_ids
        hot = hot.astype(BF16)
        store(lanes_ref, t, total, width, child, -(dot(hot, hi) + dot(hot, lo)), late)


def unpack_kernel(t, tab, s_ref, near_a, near_b, below_ref, above_ref, across_ref, lanes_ref):
    rows, width = near_a.shape[1:]
    total = rows * t.children
    me = tab[t.me]
    z = me // PLANE
    for flip in range(PLANE):
        child = me ^ flip
        here = slots(tab, t, s_ref, child, me, rows, s_ref.shape[2]) >= 0
        value = (near_a, near_b)[flip // 2][flip % 2]
        store(lanes_ref, t, total, width, child, jnp.where(here, -value, 0.0))

    @pl.when(z > 0)
    def _():
        unpack(t, tab, s_ref, lanes_ref, total, below_ref, z - 1)

    @pl.when(z < PLANES - 1)
    def _():
        unpack(t, tab, s_ref, lanes_ref, total, above_ref, z + 1)

    unpack(t, tab, s_ref, lanes_ref, total, across_ref, z ^ 2)


def expand_kernel(t, tab, s_ref, message, lanes_in, late_ref, out_ref, late, lanes_ref, sem):
    total, width = out_ref.shape
    lanes = lanes_ref.shape[1]
    z = tab[t.me] // PLANE
    at_end = (z == 0) | (z == PLANES - 1)
    lanes_ref[...] = lanes_in[...]

    @pl.when(at_end)
    def _():
        unpack(t, tab, s_ref, lanes_ref, total, message, z ^ 3)

    @pl.when(tab[t.over] != 0)
    def _():
        def more(k, carry):
            there = ((k == 0) & (z > 0)) | ((k == 1) & (z < PLANES - 1)) | (k == 2) | ((k == 3) & at_end)

            @pl.when(there)
            def _():
                copy = pltpu.make_async_copy(late_ref.at[k], late, sem)
                copy.start()
                copy.wait()
                plane = jnp.where(k == 0, z - 1, jnp.where(k == 1, z + 1, jnp.where(k == 2, z ^ 2, z ^ 3)))
                unpack(t, tab, s_ref, lanes_ref, total, late, plane, True)

            return carry

        lax.fori_loop(0, PLANE, more, 0)

    for k in range(width // lanes):
        out_ref[:, k * lanes : (k + 1) * lanes] = lanes_ref[k * total : (k + 1) * total, :]


def late_kernel(t, cap, tab, s_ref, values, message):
    rows = values.shape[2]
    to, flip = pl.program_id(0), pl.program_id(1)
    me = tab[t.me]
    block = jnp.where(
        to == 0,
        below(me, t.blocks),
        jnp.where(to == 1, above(me, t.blocks), jnp.where(to == 2, across(me, t.blocks), mirror(me, t.blocks))),
    )
    slot_ids = lax.broadcasted_iota(jnp.int32, (rows, cap), 1) + cap
    hot = slots(tab, t, s_ref, me ^ flip, block, rows, s_ref.shape[2]) == slot_ids
    hi, lo = split(values[0, 0])
    part = dot_t(hot.astype(BF16), hi) + dot_t(hot.astype(BF16), lo)

    @pl.when(flip == 0)
    def _():
        message[0] = part

    @pl.when(flip != 0)
    def _():
        message[0] += part


def vmem():
    return pl.BlockSpec(memory_space=pltpu.VMEM)


def smem():
    return pl.BlockSpec(memory_space=pltpu.SMEM)


def params(limit=VMEM_BYTES):
    return pltpu.CompilerParams(vmem_limit_bytes=limit)


def cost(flops, bytes_accessed):
    return pl.CostEstimate(
        flops=int(flops) // SCALE, bytes_accessed=int(bytes_accessed) // SCALE, transcendentals=0
    )


def after(x, *others):
    return lax.optimization_barrier((x, *others))[0]


def planes_body(cap, table, root_inverse, panels, diag_blocks, structure3):
    rows, total = root_inverse.shape
    children = structure3.shape[0]
    blocks = total // rows
    width = panels.shape[2]
    t = Table(children, blocks)

    def permute(x, move):
        return lax.ppermute(x, "row", [(r, move(r)) for r in range(blocks)])

    def along(x, planes, step):
        return lax.ppermute(
            x, "row", [(p * PLANE + b, (p + step) * PLANE + b) for p in planes for b in range(PLANE)]
        )

    def mirrored(x):
        ends = (0, PLANES - 1)
        return lax.ppermute(
            x, "row", [(p * PLANE + b, (PLANES - 1 - p) * PLANE + b) for p in ends for b in range(PLANE)]
        )

    def spread(flips, *given):
        unroll = 4
        shape = jax.ShapeDtypeStruct((len(flips), total, width), BF16)
        out = pl.BlockSpec((1, unroll * rows, width), lambda c, i: (c, i, 0))
        return pl.pallas_call(
            functools.partial(spread_kernel, t, flips, unroll),
            grid=(len(flips), blocks // unroll),
            out_shape=(shape, shape),
            in_specs=[smem(), vmem()] + [vmem()] * len(given),
            out_specs=(out, out),
            compiler_params=params(),
            cost_estimate=cost(8 * len(flips) * total * rows * 2 * width, 12 * len(flips) * total * width),
            name="spread",
        )(table, structure3, *given)

    def product(flips, here, deltas, factors, priors, given, summed=False, there=(), rest=None, panels=()):
        m = rows * len(given)
        message = jax.ShapeDtypeStruct((cap, width), F32)
        square = jax.ShapeDtypeStruct((width, width), F32)
        factor = jax.ShapeDtypeStruct((2, total, width), BF16)
        partial_sums = [square, square] if summed else []
        still = pl.BlockSpec((width, width), lambda c: (0, 0))
        whole = pl.BlockSpec((1, total, width), lambda c: (c, 0, 0))
        other_products = [rest] if there else []
        made = 2 if panels else 0
        return pl.pallas_call(
            functools.partial(
                product_kernel, t, flips, here, there, summed, bool(panels), deltas, cap, len(priors)
            ),
            grid=(2,),
            out_shape=[factor] * made
            + [jax.ShapeDtypeStruct((2, m, width), F32)]
            + partial_sums
            + [message] * len(deltas),
            in_specs=[smem(), vmem()]
            + [vmem()] * (len(priors) + len(given) + len(panels))
            + [pl.BlockSpec((1, rows * len(there), width), lambda c: (c, 0, 0))] * len(other_products)
            + [whole] * len(factors),
            out_specs=[whole] * made
            + [pl.BlockSpec((1, m, width), lambda c: (c, 0, 0))]
            + [still] * len(partial_sums)
            + [pl.BlockSpec((cap, width), lambda c: (0, 0))] * len(deltas),
            scratch_shapes=[pltpu.VMEM((2 * m, total), BF16)],
            compiler_params=params(),
            cost_estimate=cost(20 * m * total * width, 4 * len(given) * rows * total + 16 * total * width),
            name="product",
        )(table, structure3, *priors, *given, *panels, *other_products, *factors)

    def of_a(c):
        return jnp.minimum(c, 1)

    def of_b(c):
        return jnp.maximum(c - 2, 0)

    def final(factors_a, factors_b, third):
        a = pl.BlockSpec((1, total, width), lambda c: (of_a(c), 0, 0))
        b = pl.BlockSpec((1, total, width), lambda c: (of_b(c), 0, 0))
        return pl.pallas_call(
            functools.partial(last_kernel, t, cap),
            grid=(PLANE,),
            out_shape=(
                jax.ShapeDtypeStruct((PLANE, rows, width), F32),
                jax.ShapeDtypeStruct((cap, width), F32),
            ),
            in_specs=[smem()] + [vmem()] * 2 + [a, a, b, b],
            out_specs=(
                pl.BlockSpec((1, rows, width), lambda c: (c, 0, 0)),
                pl.BlockSpec((cap, width), lambda c: (0, 0)),
            ),
            scratch_shapes=[pltpu.VMEM((2 * rows, total), BF16)],
            compiler_params=params(LARGE_BYTES),
            cost_estimate=cost(40 * rows * total * width, 32 * total * width),
            name="last",
        )(table, structure3, third, *factors_a, *factors_b)

    def finish(kept, sibling, other, last, others, factors):
        def factor(flip):
            return pl.BlockSpec(
                (1, rows, width), lambda i, tab: (0, mirror(tab[t.me] ^ flip, blocks), 0)
            )

        first_of = pl.BlockSpec((1, width, width), lambda i, tab: (0, 0, 0))
        pieces = [pl.BlockSpec((1, rows, width), lambda i, tab: (0, 0, 0))] * PLANE
        return pl.pallas_call(
            finish_kernel,
            out_shape=jax.ShapeDtypeStruct((1, width, width), F32),
            grid_spec=pltpu.PrefetchScalarGridSpec(
                num_scalar_prefetch=1,
                grid=(1,),
                in_specs=[first_of]
                + [pl.BlockSpec((width, width), lambda i, tab: (0, 0))] * 3
                + pieces
                + [factor(flip) for flip in range(PLANE)] * 2,
                out_specs=first_of,
            ),
            compiler_params=params(),
            cost_estimate=cost(12 * rows * width * width, 40 * rows * width + 20 * width * width),
            name="finish",
        )(table, diag_blocks, kept, sibling, other, last, *others, *([factors[0]] * PLANE), *([factors[1]] * PLANE))

    first, second = (0, 1), (2, 3)
    near_to = ((1, below), (2, above))
    panel_1 = permute(panels, lambda r: r ^ 1)
    panel_2 = permute(panels, lambda r: r ^ 2)
    from_below = along(root_inverse, range(PLANES - 1), 1)
    from_above = along(root_inverse, range(1, PLANES), -1)
    factors_a = spread(first, panels, panel_1)

    below_2 = along(after(from_below, *factors_a), range(1, PLANES - 1), 1)
    above_2 = along(after(from_above, *factors_a), range(1, PLANES - 1), -1)
    near, far = (own, below, above), (across,)
    nearby = (root_inverse, from_below, from_above)
    near_a, down_a, up_a = product(first, near, near_to, factors_a, (), nearby)
    across_2 = below_2 + above_2
    middle = range(PLANE, (PLANES - 1) * PLANE)
    mirror_3 = lax.ppermute(
        after(across_2, near_a), "row", [(r, r + PLANE if r >= 2 * PLANE else r - PLANE) for r in middle]
    )
    panel_3 = permute(after(panel_2, across_2, near_a), lambda r: r ^ 1)
    far_a, kept_a, sent_a, twice_a = product(
        first, far, ((0, across),), factors_a, (), (across_2,), True, near, near_a
    )
    nearby = (root_inverse, from_below, from_above, across_2)
    hi_b, lo_b, near_b, kept_b, sent_b, down, up, twice = product(
        second, near + far, near_to + ((3, across),), (), (down_a, up_a, twice_a), nearby, True,
        panels=(after(panel_2, kept_a), panel_3),
    )
    factors_b = (hi_b, lo_b)
    got_across = permute(twice, lambda r: r ^ (2 * PLANE))
    got_below = along(up, range(PLANES - 1), 1)
    got_above = along(down, range(1, PLANES), -1)
    sibling_a = permute(after(sent_a, mirror_3), lambda r: r ^ 1)
    sibling_b = permute(after(sent_b, mirror_3), lambda r: r ^ 1)
    other = permute(kept_b + sibling_b, lambda r: r ^ 2)
    last, thrice = final(factors_a, factors_b, after(mirror_3, near_b))
    got_mirror = mirrored(after(thrice, got_below, got_above, got_across))
    others = [
        permute(last[flip : flip + 1], functools.partial(lambda flip, r: r ^ flip, flip))
        for flip in range(1, PLANE)
    ]
    child_inverse = finish(kept_a, sibling_a, other, last, others, factors_a)

    here = pl.BlockSpec((2, rows, width), lambda i: (0, 0, 0))
    flat = rows * children
    by_lanes = pl.pallas_call(
        functools.partial(unpack_kernel, t),
        grid=(1,),
        out_shape=jax.ShapeDtypeStruct((flat * (width // LANES), LANES), F32),
        in_specs=[smem(), vmem(), here, here] + [vmem()] * 3,
        out_specs=vmem(),
        compiler_params=params(),
        cost_estimate=cost(4 * flat * cap * width, 4 * (flat + 5 * cap) * width),
        name="unpack",
    )(table, structure3, near_a, near_b, got_below, got_above, got_across)

    def late(near_a, far_a, near_b, last):
        to_below, to_above, to_across = (
            jnp.concatenate([near_a[:, k * rows : (k + 1) * rows] if k < 3 else far_a,
                             near_b[:, k * rows : (k + 1) * rows]])
            for k in (1, 2, 3)
        )
        values = jnp.stack([to_below, to_above, to_across, last])
        packed = pl.pallas_call(
            functools.partial(late_kernel, t, cap),
            grid=(PLANE, PLANE),
            out_shape=jax.ShapeDtypeStruct((PLANE, cap, width), F32),
            in_specs=[smem(), vmem(), pl.BlockSpec((1, 1, rows, width), lambda k, c: (k, c, 0, 0))],
            out_specs=pl.BlockSpec((1, cap, width), lambda k, c: (k, 0, 0)),
            compiler_params=params(),
            name="late",
        )(table, structure3, values)
        return jnp.stack(
            [
                along(packed[1], range(PLANES - 1), 1),
                along(packed[0], range(1, PLANES), -1),
                permute(packed[2], lambda r: r ^ (2 * PLANE)),
                mirrored(packed[3]),
            ]
        )

    def none(*unused):
        return jnp.zeros((PLANE, cap, width), F32)

    more = lax.cond(table[t.over] != 0, late, none, after(near_a, got_mirror, child_inverse, by_lanes), far_a, near_b, last)
    block_rows = pl.pallas_call(
        functools.partial(expand_kernel, t),
        out_shape=jax.ShapeDtypeStruct((flat, width), F32),
        in_specs=[smem()] + [vmem()] * 3 + [pl.BlockSpec(memory_space=pl.ANY)],
        out_specs=vmem(),
        scratch_shapes=[
            pltpu.VMEM((cap, width), F32),
            pltpu.VMEM((flat * (width // LANES), LANES), F32),
            pltpu.SemaphoreType.DMA,
        ],
        compiler_params=params(),
        cost_estimate=cost(flat * cap * width, 8 * flat * width),
        name="expand",
    )(table, structure3, got_mirror, after(by_lanes, child_inverse), more)
    return block_rows.reshape(rows, children, width), child_inverse


def planes(root_inverse, panels, diag_blocks, structure, live):
    rows, total = root_inverse.shape
    children, padded = structure.shape
    blocks = total // rows
    positions = jnp.arange(padded, dtype=jnp.int32)
    block_of = jnp.where(positions[None, :] < live[:, None], structure // rows, blocks)
    edges = jnp.arange(blocks + 1, dtype=jnp.int32)
    first = jnp.sum((block_of[:, None, :] < edges[None, :, None]).astype(jnp.int32), axis=2)
    counts = (first[:, 1:] - first[:, :-1]).reshape(PLANES, PLANE, blocks)
    offsets = [jnp.zeros_like(counts[:, 0])]
    for c in range(PLANE):
        offsets.append(offsets[-1] + counts[:, c])
    largest = jnp.max(offsets[-1])
    offset = jnp.stack(offsets[:-1], axis=1).reshape(children, blocks)
    cap = 2 * rows
    table = jnp.concatenate(
        [
            first[:, :-1].reshape(-1),
            offset.reshape(-1),
            live,
            lax.axis_index("row").astype(jnp.int32)[None],
            (largest > cap).astype(jnp.int32)[None],
        ]
    )
    return planes_body(
        cap, table, root_inverse, panels, diag_blocks, structure.reshape(children, 1, padded)
    )


def body(root_inverse, panels, diag_blocks, structure, live):
    me = lax.axis_index("row")
    rows_here = root_inverse.shape[0]
    padded = structure.shape[1]
    width = panels.shape[2]
    total_rows = rows_here * lax.axis_size("row")
    mine = lax.dynamic_index_in_dim(structure, me, 0, keepdims=False)
    count = lax.dynamic_index_in_dim(live, me, 0, keepdims=False)
    columns = jnp.take(lax.all_gather(root_inverse, "row", axis=0, tiled=True), mine, axis=1)
    sub = jnp.take(columns, mine, axis=0)
    positions = jnp.arange(padded, dtype=jnp.int32)
    mask = (positions < count).astype(jnp.float32)
    masked = panels[0] * mask[:, None]
    off = -jnp.dot(sub, masked, precision=lax.Precision.HIGHEST) * mask[:, None]
    inner = diag_blocks[0] - jnp.dot(masked.T, off, precision=lax.Precision.HIGHEST)
    spread = jnp.zeros((total_rows, width), jnp.float32).at[mine].add(off)
    block_rows = lax.all_to_all(
        spread.reshape(total_rows, 1, width), "row", split_axis=0, concat_axis=1, tiled=True
    )
    return (block_rows, inner[None])


def solution(mesh):
    placed = (
        P(("pole", "row"), None),
        P(("pole", "row"), None, None),
        P(("pole", "row"), None, None),
        P(),
        P(),
    )
    return jax.shard_map(
        planes if mesh.shape["row"] == PLANES * PLANE else body,
        mesh=mesh,
        in_specs=placed,
        out_specs=(P(("pole", "row"), None, None), P(("pole", "row"), None, None)),
        check_vma=False,
    )
```

```python
import functools

import jax
import jax.numpy as jnp
from jax import lax
from jax.experimental import pallas as pl
from jax.experimental.pallas import tpu as pltpu
from jax.sharding import PartitionSpec as P

F32 = jnp.float32
BF16 = jnp.bfloat16
PLANES = 4
PLANE = 4
LANES = 128
SCALE = 16
VMEM_BYTES = 36 * 1024 * 1024
MIB = 1024 * 1024


def split(x):
    hi = x.astype(BF16)
    return hi, (x - hi.astype(F32)).astype(BF16)


def dot(a, b):
    return jnp.dot(a, b, preferred_element_type=F32)


def dot_t(a, b):
    return lax.dot_general(a, b, (((0,), (0,)), ((), ())), preferred_element_type=F32)


class Table:
    def __init__(self, children, blocks):
        self.children, self.blocks = children, blocks
        self.first = 0
        self.offset = children * blocks
        self.live = 2 * children * blocks
        self.me = self.live + children
        self.over = self.me + 1


def window(tab, t, s_ref, child, block, rows, padded):
    span = min(2 * rows, padded)
    begin = tab[t.first + child * t.blocks + block]
    at = pl.multiple_of(jnp.minimum((begin // rows) * rows, padded - span), rows)
    row_ids = lax.broadcasted_iota(jnp.int32, (rows, span), 0) + block * rows
    positions = lax.broadcasted_iota(jnp.int32, (rows, span), 1) + at
    hit = (row_ids == s_ref[child, :, pl.ds(at, span)]) & (positions < tab[t.live + child])
    return at, span, positions, hit


def slots(tab, t, s_ref, child, block, rows, padded):
    _, _, positions, hit = window(tab, t, s_ref, child, block, rows, padded)
    shift = tab[t.offset + child * t.blocks + block] - tab[t.first + child * t.blocks + block]
    return jnp.max(jnp.where(hit, positions + shift, -1), axis=1, keepdims=True)


def spread_block(t, tab, s_ref, child, block, rows, panel, hi_ref, lo_ref, to):
    at, span, _, hit = window(tab, t, s_ref, child, block, rows, s_ref.shape[2])
    hot = hit.astype(BF16)
    hi, lo = split(panel[0, pl.ds(at, span), :])
    hi_ref[0, to, :] = dot(hot, hi).astype(BF16)
    lo_ref[0, to, :] = dot(hot, lo).astype(BF16)


def spread_kernel(t, flips, unroll, tab, s_ref, *refs):
    panels, (hi_ref, lo_ref) = refs[: len(flips)], refs[len(flips) :]
    rows = hi_ref.shape[1] // unroll
    for c, flip in enumerate(flips):

        @pl.when(pl.program_id(0) == c)
        def _():
            child = tab[t.me] ^ flip
            for u in range(unroll):
                block = pl.program_id(1) * unroll + u
                to = slice(u * rows, (u + 1) * rows)
                spread_block(t, tab, s_ref, child, block, rows, panels[c], hi_ref, lo_ref, to)


def product_kernel(t, flips, here, there, summed, spreads, deltas, cap, prior, tab, s_ref, *refs):
    count = len(here)
    priors, blocks, refs = refs[:prior], refs[prior : prior + count], refs[prior + count :]
    if spreads:
        panels, refs = refs[:2], refs[2:]
    if there:
        rest_ref, refs = refs[0], refs[1:]
    hi_ref, lo_ref, out_ref, refs = refs[0], refs[1], refs[2], refs[3:]
    if summed:
        kept_ref, sent_ref, refs = refs[0], refs[1], refs[2:]
    messages, x_ref = refs[:-1], refs[-1]
    rows = blocks[0].shape[0]
    m = rows * count
    padded = s_ref.shape[2]
    me = tab[t.me]
    step = pl.program_id(0)

    @pl.when(step == 0)
    def _():
        for k in range(count):
            hi, lo = split(blocks[k][...])
            x_ref[pl.ds(k * rows, rows), :] = hi
            x_ref[pl.ds(m + k * rows, rows), :] = lo

    if spreads:
        for c, flip in enumerate(flips):

            @pl.when(step == c)
            def _(panel=panels[c], flip=flip):
                for block in range(t.blocks):
                    to = slice(block * rows, (block + 1) * rows)
                    spread_block(t, tab, s_ref, me ^ flip, block, rows, panel, hi_ref, lo_ref, to)

    both = dot(x_ref[...], hi_ref[0])
    product = both[:m] + both[m:] + dot(x_ref[:m, :], lo_ref[0])
    out_ref[0] = product
    child = me ^ jnp.where(step == 0, flips[0], flips[1])
    slot_ids = lax.broadcasted_iota(jnp.int32, (rows, cap), 1)
    for n, (message, (k, delta)) in enumerate(zip(messages, deltas)):
        hot = slots(tab, t, s_ref, child, delta(me, t.blocks), rows, padded) == slot_ids
        hi, lo = split(product[k * rows : (k + 1) * rows])
        part = dot_t(hot.astype(BF16), hi) + dot_t(hot.astype(BF16), lo)

        @pl.when(step == 0)
        def _(n=n, message=message, part=part):
            message[...] = part + priors[n][...] if prior else part

        @pl.when(step != 0)
        def _(message=message, part=part):
            message[...] += part

    if summed:
        values = jnp.concatenate([product, rest_ref[0]], axis=0) if there else product
        at = [pl.multiple_of(delta(me, t.blocks) * rows, rows) for delta in here + there]
        bh = jnp.concatenate([hi_ref[0, pl.ds(k, rows), :] for k in at], axis=0)
        bl = jnp.concatenate([lo_ref[0, pl.ds(k, rows), :] for k in at], axis=0)
        hi, lo = split(values)
        inner = dot_t(bh, hi) + dot_t(bh, lo) + dot_t(bl, hi)

        @pl.when(step == 0)
        def _():
            kept_ref[...] = inner

        @pl.when(step != 0)
        def _():
            sent_ref[...] = inner


def last_kernel(t, cap, tab, s_ref, third_ref, hi_a, lo_a, hi_b, lo_b, *refs):
    outs, (message, x_ref) = refs[:PLANE], refs[PLANE:]
    rows = third_ref.shape[0]
    padded = s_ref.shape[2]
    me = tab[t.me]
    step = pl.program_id(0)

    @pl.when(step == 0)
    def _():
        hi, lo = split(third_ref[...])
        x_ref[:rows, :] = hi
        x_ref[rows:, :] = lo

    slot_ids = lax.broadcasted_iota(jnp.int32, (rows, cap), 1)
    for flip, (hi_ref, lo_ref) in enumerate(((hi_a, lo_a), (hi_a, lo_a), (hi_b, lo_b), (hi_b, lo_b))):

        @pl.when(step == flip)
        def _(flip=flip, hi_ref=hi_ref, lo_ref=lo_ref):
            both = dot(x_ref[...], hi_ref[0])
            product = both[:rows] + both[rows:] + dot(x_ref[:rows, :], lo_ref[0])
            outs[flip][0] = product
            hot = slots(tab, t, s_ref, me ^ flip, mirror(me, t.blocks), rows, padded) == slot_ids
            hi, lo = split(product)
            part = dot_t(hot.astype(BF16), hi) + dot_t(hot.astype(BF16), lo)
            to = slice(flip // 2 * cap, flip // 2 * cap + cap)
            if flip % 2 == 0:
                message[to, :] = part
            else:
                message[to, :] += part


def finish_kernel(tab, diag_ref, kept_ref, sibling_ref, other_ref, *refs):
    products, (factors_hi, factors_lo, out_ref) = refs[:4], (refs[4:8], refs[8:12], refs[12])
    hi, lo = split(jnp.concatenate([g[0] for g in products], axis=0))
    bh = jnp.concatenate([b[0] for b in factors_hi], axis=0)
    bl = jnp.concatenate([b[0] for b in factors_lo], axis=0)
    added = dot_t(bh, hi) + dot_t(bh, lo) + dot_t(bl, hi)
    out_ref[0] = diag_ref[0] + (kept_ref[...] + sibling_ref[...] + other_ref[...] + added)


def own(me, blocks):
    return me


def below(me, blocks):
    return jnp.maximum(me - PLANE, 0)


def above(me, blocks):
    return jnp.minimum(me + PLANE, blocks - 1)


def across(me, blocks):
    return me ^ (2 * PLANE)


def mirror(me, blocks):
    return me ^ (3 * PLANE)


def store(lanes_ref, t, total, width, child, value, late=0):
    lanes = lanes_ref.shape[1]
    for k in range(width // lanes):
        to = pl.ds(k * total + child, total // t.children, stride=t.children)
        part = value[:, k * lanes : (k + 1) * lanes]
        lanes_ref[to, :] = lanes_ref[to, :] + part if late else part


def unpack(t, tab, s_ref, lanes_ref, total, message, plane, half, late=0):
    cap, width = message.shape
    rows = total // t.children
    me = tab[t.me]
    slot_ids = lax.broadcasted_iota(jnp.int32, (rows, cap), 1) + late
    hi, lo = split(message[...])
    first = plane * PLANE + ((me % PLANE) ^ (2 * half)) // 2 * 2
    for c in range(2):
        hot = slots(tab, t, s_ref, first + c, me, rows, s_ref.shape[2]) == slot_ids
        hot = hot.astype(BF16)
        store(lanes_ref, t, total, width, first + c, -(dot(hot, hi) + dot(hot, lo)), late)


def unpack_kernel(t, tab, s_ref, near_a, near_b, *refs):
    messages, lanes_ref = refs[:-1], refs[-1]
    rows, width = near_a.shape[1:]
    total = rows * t.children
    me = tab[t.me]
    z = me // PLANE
    for flip in range(PLANE):
        child = me ^ flip
        here = slots(tab, t, s_ref, child, me, rows, s_ref.shape[2]) >= 0
        value = (near_a, near_b)[flip // 2][flip % 2]
        store(lanes_ref, t, total, width, child, jnp.where(here, -value, 0.0))
    for half in range(2):
        below_ref, above_ref, across_ref = messages[3 * half : 3 * half + 3]

        @pl.when(z > 0)
        def _(below_ref=below_ref, half=half):
            unpack(t, tab, s_ref, lanes_ref, total, below_ref, z - 1, half)

        @pl.when(z < PLANES - 1)
        def _(above_ref=above_ref, half=half):
            unpack(t, tab, s_ref, lanes_ref, total, above_ref, z + 1, half)

        unpack(t, tab, s_ref, lanes_ref, total, across_ref, z ^ 2, half)


def expand_kernel(t, tab, s_ref, message, lanes_in, late_ref, out_ref, late, lanes_ref, sem):
    total, width = out_ref.shape
    lanes = lanes_ref.shape[1]
    cap, more = message.shape[0] // 2, late.shape[0] // 2
    z = tab[t.me] // PLANE
    at_end = (z == 0) | (z == PLANES - 1)
    whole = pltpu.make_async_copy(lanes_in, lanes_ref, sem)
    whole.start()
    whole.wait()

    @pl.when(at_end)
    def _():
        for half in range(2):
            part = message.at[half * cap : half * cap + cap, :]
            unpack(t, tab, s_ref, lanes_ref, total, part, z ^ 3, half)

    @pl.when(tab[t.over] != 0)
    def _():
        def step(k, carry):
            there = ((k == 0) & (z > 0)) | ((k == 1) & (z < PLANES - 1)) | (k == 2) | ((k == 3) & at_end)

            @pl.when(there)
            def _():
                copy = pltpu.make_async_copy(late_ref.at[k], late, sem)
                copy.start()
                copy.wait()
                plane = jnp.where(k == 0, z - 1, jnp.where(k == 1, z + 1, jnp.where(k == 2, z ^ 2, z ^ 3)))
                for half in range(2):
                    part = late.at[half * more : half * more + more, :]
                    unpack(t, tab, s_ref, lanes_ref, total, part, plane, half, cap)

            return carry

        lax.fori_loop(0, PLANE, step, 0)

    for k in range(width // lanes):
        out_ref[:, k * lanes : (k + 1) * lanes] = lanes_ref[k * total : (k + 1) * total, :]


def late_kernel(t, cap, tab, s_ref, values, message):
    rows = values.shape[2]
    to, flip = pl.program_id(0), pl.program_id(1)
    me = tab[t.me]
    block = jnp.where(
        to == 0,
        below(me, t.blocks),
        jnp.where(to == 1, above(me, t.blocks), jnp.where(to == 2, across(me, t.blocks), mirror(me, t.blocks))),
    )
    more = message.shape[1] // 2
    slot_ids = lax.broadcasted_iota(jnp.int32, (rows, more), 1) + cap
    hot = slots(tab, t, s_ref, me ^ flip, block, rows, s_ref.shape[2]) == slot_ids
    hi, lo = split(values[0, 0])
    part = dot_t(hot.astype(BF16), hi) + dot_t(hot.astype(BF16), lo)
    for half in range(2):
        at = slice(half * more, half * more + more)

        @pl.when(flip == 2 * half)
        def _(at=at):
            message[0, at, :] = part

        @pl.when(flip == 2 * half + 1)
        def _(at=at):
            message[0, at, :] += part


def vmem():
    return pl.BlockSpec(memory_space=pltpu.VMEM)


def smem():
    return pl.BlockSpec(memory_space=pltpu.SMEM)


def params(limit=VMEM_BYTES):
    return pltpu.CompilerParams(vmem_limit_bytes=limit)


def cost(flops, bytes_accessed):
    return pl.CostEstimate(
        flops=int(flops) // SCALE, bytes_accessed=int(bytes_accessed) // SCALE, transcendentals=0
    )


def after(x, *others):
    return lax.optimization_barrier((x, *others))[0]


def planes_body(cap, table, root_inverse, panels, diag_blocks, structure3):
    rows, total = root_inverse.shape
    children = structure3.shape[0]
    blocks = total // rows
    width = panels.shape[2]
    t = Table(children, blocks)

    def permute(x, move):
        return lax.ppermute(x, "row", [(r, move(r)) for r in range(blocks)])

    def along(x, planes, step):
        return lax.ppermute(
            x, "row", [(p * PLANE + b, (p + step) * PLANE + b) for p in planes for b in range(PLANE)]
        )

    def mirrored(x):
        ends = (0, PLANES - 1)
        return lax.ppermute(
            x, "row", [(p * PLANE + b, (PLANES - 1 - p) * PLANE + b) for p in ends for b in range(PLANE)]
        )

    def spread(flips, *given):
        unroll = 4
        shape = jax.ShapeDtypeStruct((len(flips), total, width), BF16)
        out = pl.BlockSpec((1, unroll * rows, width), lambda c, i: (c, i, 0))
        return pl.pallas_call(
            functools.partial(spread_kernel, t, flips, unroll),
            grid=(len(flips), blocks // unroll),
            out_shape=(shape, shape),
            in_specs=[smem(), vmem()] + [vmem()] * len(given),
            out_specs=(out, out),
            compiler_params=params(16 * MIB),
            cost_estimate=cost(8 * len(flips) * total * rows * 2 * width, 12 * len(flips) * total * width),
            name="spread",
        )(table, structure3, *given)

    def product(flips, here, deltas, factors, priors, given, summed=False, there=(), rest=None, panels=()):
        m = rows * len(given)
        message = jax.ShapeDtypeStruct((cap, width), F32)
        square = jax.ShapeDtypeStruct((width, width), F32)
        factor = jax.ShapeDtypeStruct((2, total, width), BF16)
        partial_sums = [square, square] if summed else []
        still = pl.BlockSpec((width, width), lambda c: (0, 0))
        whole = pl.BlockSpec((1, total, width), lambda c: (c, 0, 0))
        other_products = [rest] if there else []
        made = 2 if panels else 0
        return pl.pallas_call(
            functools.partial(
                product_kernel, t, flips, here, there, summed, bool(panels), deltas, cap, len(priors)
            ),
            grid=(2,),
            out_shape=[factor] * made
            + [jax.ShapeDtypeStruct((2, m, width), F32)]
            + partial_sums
            + [message] * len(deltas),
            in_specs=[smem(), vmem()]
            + [vmem()] * (len(priors) + len(given) + len(panels))
            + [pl.BlockSpec((1, rows * len(there), width), lambda c: (c, 0, 0))] * len(other_products)
            + [whole] * len(factors),
            out_specs=[whole] * made
            + [pl.BlockSpec((1, m, width), lambda c: (c, 0, 0))]
            + [still] * len(partial_sums)
            + [pl.BlockSpec((cap, width), lambda c: (0, 0))] * len(deltas),
            scratch_shapes=[pltpu.VMEM((2 * m, total), BF16)],
            compiler_params=params(28 * MIB),
            cost_estimate=cost(20 * m * total * width, 4 * len(given) * rows * total + 16 * total * width),
            name="product",
        )(table, structure3, *priors, *given, *panels, *other_products, *factors)

    def of_a(c):
        return jnp.minimum(c, 1)

    def of_b(c):
        return jnp.maximum(c - 2, 0)

    def final(factors_a, factors_b, third):
        a = pl.BlockSpec((1, total, width), lambda c: (of_a(c), 0, 0))
        b = pl.BlockSpec((1, total, width), lambda c: (of_b(c), 0, 0))
        return pl.pallas_call(
            functools.partial(last_kernel, t, cap),
            grid=(PLANE,),
            out_shape=(
                *[jax.ShapeDtypeStruct((1, rows, width), F32)] * PLANE,
                jax.ShapeDtypeStruct((2 * cap, width), F32),
            ),
            in_specs=[smem()] + [vmem()] * 2 + [a, a, b, b],
            out_specs=(
                *[pl.BlockSpec((1, rows, width), lambda c: (0, 0, 0))] * PLANE,
                pl.BlockSpec((2 * cap, width), lambda c: (0, 0)),
            ),
            scratch_shapes=[pltpu.VMEM((2 * rows, total), BF16)],
            compiler_params=params(20 * MIB),
            cost_estimate=cost(40 * rows * total * width, 32 * total * width),
            name="last",
        )(table, structure3, third, *factors_a, *factors_b)

    def finish(kept, sibling, other, last, others, factors):
        def factor(flip):
            return pl.BlockSpec(
                (1, rows, width), lambda i, tab: (0, mirror(tab[t.me] ^ flip, blocks), 0)
            )

        first_of = pl.BlockSpec((1, width, width), lambda i, tab: (0, 0, 0))
        pieces = [pl.BlockSpec((1, rows, width), lambda i, tab: (0, 0, 0))] * PLANE
        return pl.pallas_call(
            finish_kernel,
            out_shape=jax.ShapeDtypeStruct((1, width, width), F32),
            grid_spec=pltpu.PrefetchScalarGridSpec(
                num_scalar_prefetch=1,
                grid=(1,),
                in_specs=[first_of]
                + [pl.BlockSpec((width, width), lambda i, tab: (0, 0))] * 3
                + pieces
                + [factor(flip) for flip in range(PLANE)] * 2,
                out_specs=first_of,
            ),
            compiler_params=params(12 * MIB),
            cost_estimate=cost(12 * rows * width * width, 40 * rows * width + 20 * width * width),
            name="finish",
        )(table, diag_blocks, kept, sibling, other, last[0], *others, *([factors[0]] * PLANE), *([factors[1]] * PLANE))

    first, second = (0, 1), (2, 3)
    near_to = ((1, below), (2, above))
    panel_1 = permute(panels, lambda r: r ^ 1)
    panel_2 = permute(panels, lambda r: r ^ 2)
    from_below = along(root_inverse, range(PLANES - 1), 1)
    from_above = along(root_inverse, range(1, PLANES), -1)
    factors_a = spread(first, panels, panel_1)

    below_2 = along(after(from_below, *factors_a), range(1, PLANES - 1), 1)
    above_2 = along(after(from_above, *factors_a), range(1, PLANES - 1), -1)
    near, far = (own, below, above), (across,)
    nearby = (root_inverse, from_below, from_above)
    near_a, down_a, up_a = product(first, near, near_to, factors_a, (), nearby)
    across_2 = below_2 + above_2
    middle = range(PLANE, (PLANES - 1) * PLANE)
    mirror_3 = lax.ppermute(
        after(across_2, near_a), "row", [(r, r + PLANE if r >= 2 * PLANE else r - PLANE) for r in middle]
    )
    panel_3 = permute(after(panel_2, across_2, near_a), lambda r: r ^ 1)
    got_below_a = along(up_a, range(PLANES - 1), 1)
    got_above_a = along(down_a, range(1, PLANES), -1)
    far_a, kept_a, sent_a, twice_a = product(
        first, far, ((0, across),), factors_a, (), (across_2,), True, near, near_a
    )
    got_across_a = permute(twice_a, lambda r: r ^ (2 * PLANE))
    early = (got_below_a, got_above_a, got_across_a)
    nearby = (root_inverse, from_below, from_above, across_2)
    hi_b, lo_b, near_b, kept_b, sent_b, down, up, twice = product(
        second, near + far, near_to + ((3, across),), (), (), nearby, True,
        panels=(after(panel_2, kept_a), panel_3),
    )
    factors_b = (hi_b, lo_b)
    got_across = permute(twice, lambda r: r ^ (2 * PLANE))
    got_below = along(up, range(PLANES - 1), 1)
    got_above = along(down, range(1, PLANES), -1)
    sibling_a = permute(after(sent_a, mirror_3, *early), lambda r: r ^ 1)
    sibling_b = permute(after(sent_b, mirror_3, *early), lambda r: r ^ 1)
    other = permute(kept_b + sibling_b, lambda r: r ^ 2)
    *last, thrice = final(factors_a, factors_b, after(mirror_3, near_b))
    got_mirror = mirrored(after(thrice, got_below, got_above, got_across))
    others = [
        permute(last[flip], functools.partial(lambda flip, r: r ^ flip, flip))
        for flip in range(1, PLANE)
    ]
    child_inverse = finish(kept_a, sibling_a, other, last, others, factors_a)

    here = pl.BlockSpec((2, rows, width), lambda i: (0, 0, 0))
    flat = rows * children
    by_lanes = pl.pallas_call(
        functools.partial(unpack_kernel, t),
        grid=(1,),
        out_shape=jax.ShapeDtypeStruct((flat * (width // LANES), LANES), F32),
        in_specs=[smem(), vmem(), here, here] + [vmem()] * 6,
        out_specs=vmem(),
        compiler_params=params(16 * MIB),
        cost_estimate=cost(4 * flat * cap * width, 4 * (flat + 5 * cap) * width),
        name="unpack",
    )(table, structure3, near_a, near_b, *early, got_below, got_above, got_across)

    more = 2 * rows - cap

    def late(near_a, far_a, near_b, *last):
        to_below, to_above, to_across = (
            jnp.concatenate([near_a[:, k * rows : (k + 1) * rows] if k < 3 else far_a,
                             near_b[:, k * rows : (k + 1) * rows]])
            for k in (1, 2, 3)
        )
        values = jnp.stack([to_below, to_above, to_across, jnp.concatenate(last)])
        packed = pl.pallas_call(
            functools.partial(late_kernel, t, cap),
            grid=(PLANE, PLANE),
            out_shape=jax.ShapeDtypeStruct((PLANE, 2 * more, width), F32),
            in_specs=[smem(), vmem(), pl.BlockSpec((1, 1, rows, width), lambda k, c: (k, c, 0, 0))],
            out_specs=pl.BlockSpec((1, 2 * more, width), lambda k, c: (k, 0, 0)),
            compiler_params=params(16 * MIB),
            name="late",
        )(table, structure3, values)
        return jnp.stack(
            [
                along(packed[1], range(PLANES - 1), 1),
                along(packed[0], range(1, PLANES), -1),
                permute(packed[2], lambda r: r ^ (2 * PLANE)),
                mirrored(packed[3]),
            ]
        )

    def none(*unused):
        return jnp.zeros((PLANE, 2 * more, width), F32)

    beyond = lax.cond(table[t.over] != 0, late, none, after(near_a, got_mirror, child_inverse, by_lanes), far_a, near_b, *last)
    block_rows = pl.pallas_call(
        functools.partial(expand_kernel, t),
        out_shape=jax.ShapeDtypeStruct((flat, width), F32),
        in_specs=[smem()] + [vmem()] * 2 + [pl.BlockSpec(memory_space=pl.ANY)] * 2,
        out_specs=vmem(),
        scratch_shapes=[
            pltpu.VMEM((2 * more, width), F32),
            pltpu.VMEM((flat * (width // LANES), LANES), F32),
            pltpu.SemaphoreType.DMA,
        ],
        compiler_params=params(16 * MIB),
        cost_estimate=cost(flat * cap * width, 8 * flat * width),
        name="expand",
    )(table, structure3, got_mirror, after(by_lanes, child_inverse), beyond)
    return block_rows.reshape(rows, children, width), child_inverse


def planes(root_inverse, panels, diag_blocks, structure, live):
    rows, total = root_inverse.shape
    children, padded = structure.shape
    blocks = total // rows
    positions = jnp.arange(padded, dtype=jnp.int32)
    block_of = jnp.where(positions[None, :] < live[:, None], structure // rows, blocks)
    edges = jnp.arange(blocks + 1, dtype=jnp.int32)
    first = jnp.sum((block_of[:, None, :] < edges[None, :, None]).astype(jnp.int32), axis=2)
    counts = (first[:, 1:] - first[:, :-1]).reshape(children // 2, 2, blocks)
    largest = jnp.max(counts[:, 0] + counts[:, 1])
    offset = jnp.stack([jnp.zeros_like(counts[:, 0]), counts[:, 0]], axis=1).reshape(children, blocks)
    cap = rows + rows // 8
    table = jnp.concatenate(
        [
            first[:, :-1].reshape(-1),
            offset.reshape(-1),
            live,
            lax.axis_index("row").astype(jnp.int32)[None],
            (largest > cap).astype(jnp.int32)[None],
        ]
    )
    return planes_body(
        cap, table, root_inverse, panels, diag_blocks, structure.reshape(children, 1, padded)
    )


def body(root_inverse, panels, diag_blocks, structure, live):
    me = lax.axis_index("row")
    rows_here = root_inverse.shape[0]
    padded = structure.shape[1]
    width = panels.shape[2]
    total_rows = rows_here * lax.axis_size("row")
    mine = lax.dynamic_index_in_dim(structure, me, 0, keepdims=False)
    count = lax.dynamic_index_in_dim(live, me, 0, keepdims=False)
    columns = jnp.take(lax.all_gather(root_inverse, "row", axis=0, tiled=True), mine, axis=1)
    sub = jnp.take(columns, mine, axis=0)
    positions = jnp.arange(padded, dtype=jnp.int32)
    mask = (positions < count).astype(jnp.float32)
    masked = panels[0] * mask[:, None]
    off = -jnp.dot(sub, masked, precision=lax.Precision.HIGHEST) * mask[:, None]
    inner = diag_blocks[0] - jnp.dot(masked.T, off, precision=lax.Precision.HIGHEST)
    spread = jnp.zeros((total_rows, width), jnp.float32).at[mine].add(off)
    block_rows = lax.all_to_all(
        spread.reshape(total_rows, 1, width), "row", split_axis=0, concat_axis=1, tiled=True
    )
    return (block_rows, inner[None])


def solution(mesh):
    placed = (
        P(("pole", "row"), None),
        P(("pole", "row"), None, None),
        P(("pole", "row"), None, None),
        P(),
        P(),
    )
    return jax.shard_map(
        planes if mesh.shape["row"] == PLANES * PLANE else body,
        mesh=mesh,
        in_specs=placed,
        out_specs=(P(("pole", "row"), None, None), P(("pole", "row"), None, None)),
        check_vma=False,
    )
```

```python
import functools

import jax
import jax.numpy as jnp
from jax import lax
from jax.experimental import pallas as pl
from jax.experimental.pallas import tpu as pltpu
from jax.sharding import PartitionSpec as P

F32 = jnp.float32
BF16 = jnp.bfloat16
PLANES = 4
PLANE = 4
LANES = 128
SCALE = 16
VMEM_BYTES = 36 * 1024 * 1024
MIB = 1024 * 1024


def split(x):
    hi = x.astype(BF16)
    return hi, (x - hi.astype(F32)).astype(BF16)


def dot(a, b):
    return jnp.dot(a, b, preferred_element_type=F32)


def dot_t(a, b):
    return lax.dot_general(a, b, (((0,), (0,)), ((), ())), preferred_element_type=F32)


class Table:
    def __init__(self, children, blocks):
        self.children, self.blocks = children, blocks
        self.first = 0
        self.offset = children * blocks
        self.live = 2 * children * blocks
        self.me = self.live + children
        self.over = self.me + 1


def window(tab, t, s_ref, child, block, rows, padded):
    span = min(2 * rows, padded)
    begin = tab[t.first + child * t.blocks + block]
    at = pl.multiple_of(jnp.minimum((begin // rows) * rows, padded - span), rows)
    row_ids = lax.broadcasted_iota(jnp.int32, (rows, span), 0) + block * rows
    positions = lax.broadcasted_iota(jnp.int32, (rows, span), 1) + at
    hit = (row_ids == s_ref[child, :, pl.ds(at, span)]) & (positions < tab[t.live + child])
    return at, span, positions, hit


def slots(tab, t, s_ref, child, block, rows, padded):
    _, _, positions, hit = window(tab, t, s_ref, child, block, rows, padded)
    shift = tab[t.offset + child * t.blocks + block] - tab[t.first + child * t.blocks + block]
    return jnp.max(jnp.where(hit, positions + shift, -1), axis=1, keepdims=True)


def spread_block(t, tab, s_ref, child, block, rows, panel, hi_ref, lo_ref, to):
    at, span, _, hit = window(tab, t, s_ref, child, block, rows, s_ref.shape[2])
    hot = hit.astype(BF16)
    hi, lo = split(panel[0, pl.ds(at, span), :])
    hi_ref[0, to, :] = dot(hot, hi).astype(BF16)
    lo_ref[0, to, :] = dot(hot, lo).astype(BF16)


def spread_kernel(t, flips, unroll, tab, s_ref, *refs):
    panels, (hi_ref, lo_ref) = refs[: len(flips)], refs[len(flips) :]
    rows = hi_ref.shape[1] // unroll
    for c, flip in enumerate(flips):

        @pl.when(pl.program_id(0) == c)
        def _():
            child = tab[t.me] ^ flip
            for u in range(unroll):
                block = pl.program_id(1) * unroll + u
                to = slice(u * rows, (u + 1) * rows)
                spread_block(t, tab, s_ref, child, block, rows, panels[c], hi_ref, lo_ref, to)


def product_kernel(t, flips, here, there, summed, spreads, deltas, cap, prior, tab, s_ref, *refs):
    count = len(here)
    priors, blocks, refs = refs[:prior], refs[prior : prior + count], refs[prior + count :]
    if spreads:
        panels, refs = refs[:2], refs[2:]
    if there:
        rest_ref, refs = refs[0], refs[1:]
    hi_ref, lo_ref, out_ref, refs = refs[0], refs[1], refs[2], refs[3:]
    if summed:
        kept_ref, sent_ref, refs = refs[0], refs[1], refs[2:]
    messages, x_ref = refs[:-1], refs[-1]
    rows = blocks[0].shape[0]
    m = rows * count
    padded = s_ref.shape[2]
    me = tab[t.me]
    step = pl.program_id(0)

    @pl.when(step == 0)
    def _():
        for k in range(count):
            hi, lo = split(blocks[k][...])
            x_ref[pl.ds(k * rows, rows), :] = hi
            x_ref[pl.ds(m + k * rows, rows), :] = lo

    if spreads:
        for c, flip in enumerate(flips):

            @pl.when(step == c)
            def _(panel=panels[c], flip=flip):
                for block in range(t.blocks):
                    to = slice(block * rows, (block + 1) * rows)
                    spread_block(t, tab, s_ref, me ^ flip, block, rows, panel, hi_ref, lo_ref, to)

    both = dot(x_ref[...], hi_ref[0])
    product = both[:m] + both[m:] + dot(x_ref[:m, :], lo_ref[0])
    out_ref[0] = product
    child = me ^ jnp.where(step == 0, flips[0], flips[1])
    slot_ids = lax.broadcasted_iota(jnp.int32, (rows, cap), 1)
    for n, (message, (k, delta)) in enumerate(zip(messages, deltas)):
        hot = slots(tab, t, s_ref, child, delta(me, t.blocks), rows, padded) == slot_ids
        hi, lo = split(product[k * rows : (k + 1) * rows])
        part = dot_t(hot.astype(BF16), hi) + dot_t(hot.astype(BF16), lo)

        @pl.when(step == 0)
        def _(n=n, message=message, part=part):
            message[...] = part + priors[n][...] if prior else part

        @pl.when(step != 0)
        def _(message=message, part=part):
            message[...] += part

    if summed:
        values = jnp.concatenate([product, rest_ref[0]], axis=0) if there else product
        at = [pl.multiple_of(delta(me, t.blocks) * rows, rows) for delta in here + there]
        bh = jnp.concatenate([hi_ref[0, pl.ds(k, rows), :] for k in at], axis=0)
        bl = jnp.concatenate([lo_ref[0, pl.ds(k, rows), :] for k in at], axis=0)
        hi, lo = split(values)
        inner = dot_t(bh, hi) + dot_t(bh, lo) + dot_t(bl, hi)

        @pl.when(step == 0)
        def _():
            kept_ref[...] = inner

        @pl.when(step != 0)
        def _():
            sent_ref[...] = inner


def last_kernel(t, cap, tab, s_ref, third_ref, hi_a, lo_a, hi_b, lo_b, *refs):
    outs, (message, x_ref) = refs[:PLANE], refs[PLANE:]
    rows = third_ref.shape[0]
    padded = s_ref.shape[2]
    me = tab[t.me]
    step = pl.program_id(0)

    @pl.when(step == 0)
    def _():
        hi, lo = split(third_ref[...])
        x_ref[:rows, :] = hi
        x_ref[rows:, :] = lo

    slot_ids = lax.broadcasted_iota(jnp.int32, (rows, cap), 1)
    for flip, (hi_ref, lo_ref) in enumerate(((hi_a, lo_a), (hi_a, lo_a), (hi_b, lo_b), (hi_b, lo_b))):

        @pl.when(step == flip)
        def _(flip=flip, hi_ref=hi_ref, lo_ref=lo_ref):
            both = dot(x_ref[...], hi_ref[0])
            product = both[:rows] + both[rows:] + dot(x_ref[:rows, :], lo_ref[0])
            outs[flip][0] = product
            hot = slots(tab, t, s_ref, me ^ flip, mirror(me, t.blocks), rows, padded) == slot_ids
            hi, lo = split(product)
            part = dot_t(hot.astype(BF16), hi) + dot_t(hot.astype(BF16), lo)
            to = slice(flip // 2 * cap, flip // 2 * cap + cap)
            if flip % 2 == 0:
                message[to, :] = part
            else:
                message[to, :] += part


def finish_kernel(tab, diag_ref, kept_ref, sibling_ref, other_ref, *refs):
    products, (factors_hi, factors_lo, out_ref) = refs[:4], (refs[4:8], refs[8:12], refs[12])
    hi, lo = split(jnp.concatenate([g[0] for g in products], axis=0))
    bh = jnp.concatenate([b[0] for b in factors_hi], axis=0)
    bl = jnp.concatenate([b[0] for b in factors_lo], axis=0)
    added = dot_t(bh, hi) + dot_t(bh, lo) + dot_t(bl, hi)
    out_ref[0] = diag_ref[0] + (kept_ref[...] + sibling_ref[...] + other_ref[...] + added)


def own(me, blocks):
    return me


def below(me, blocks):
    return jnp.maximum(me - PLANE, 0)


def above(me, blocks):
    return jnp.minimum(me + PLANE, blocks - 1)


def across(me, blocks):
    return me ^ (2 * PLANE)


def mirror(me, blocks):
    return me ^ (3 * PLANE)


def store(lanes_ref, t, total, width, child, value, late=0):
    lanes = lanes_ref.shape[1]
    for k in range(width // lanes):
        to = pl.ds(k * total + child, total // t.children, stride=t.children)
        part = value[:, k * lanes : (k + 1) * lanes]
        lanes_ref[to, :] = lanes_ref[to, :] + part if late else part


def unpack(t, tab, s_ref, lanes_ref, total, message, plane, half, late=0):
    cap, width = message.shape
    rows = total // t.children
    me = tab[t.me]
    slot_ids = lax.broadcasted_iota(jnp.int32, (rows, cap), 1) + late
    hi, lo = split(message[...])
    first = plane * PLANE + ((me % PLANE) ^ (2 * half)) // 2 * 2
    for c in range(2):
        hot = slots(tab, t, s_ref, first + c, me, rows, s_ref.shape[2]) == slot_ids
        hot = hot.astype(BF16)
        store(lanes_ref, t, total, width, first + c, -(dot(hot, hi) + dot(hot, lo)), late)


def unpack_kernel(t, tab, s_ref, near_a, near_b, *refs):
    messages, lanes_ref = refs[:-1], refs[-1]
    rows, width = near_a.shape[1:]
    total = rows * t.children
    me = tab[t.me]
    z = me // PLANE
    for flip in range(PLANE):
        child = me ^ flip
        here = slots(tab, t, s_ref, child, me, rows, s_ref.shape[2]) >= 0
        value = (near_a, near_b)[flip // 2][flip % 2]
        store(lanes_ref, t, total, width, child, jnp.where(here, -value, 0.0))
    for half in range(2):
        below_ref, above_ref, across_ref = messages[3 * half : 3 * half + 3]

        @pl.when(z > 0)
        def _(below_ref=below_ref, half=half):
            unpack(t, tab, s_ref, lanes_ref, total, below_ref, z - 1, half)

        @pl.when(z < PLANES - 1)
        def _(above_ref=above_ref, half=half):
            unpack(t, tab, s_ref, lanes_ref, total, above_ref, z + 1, half)

        unpack(t, tab, s_ref, lanes_ref, total, across_ref, z ^ 2, half)


def expand_kernel(t, tab, s_ref, message, lanes_in, late_ref, out_ref, late, lanes_ref, sem):
    total, width = out_ref.shape
    lanes = lanes_ref.shape[1]
    cap, more = message.shape[0] // 2, late.shape[0] // 2
    z = tab[t.me] // PLANE
    at_end = (z == 0) | (z == PLANES - 1)
    whole = pltpu.make_async_copy(lanes_in, lanes_ref, sem)
    whole.start()
    whole.wait()

    @pl.when(at_end)
    def _():
        for half in range(2):
            part = message.at[half * cap : half * cap + cap, :]
            unpack(t, tab, s_ref, lanes_ref, total, part, z ^ 3, half)

    @pl.when(tab[t.over] != 0)
    def _():
        def step(k, carry):
            there = ((k == 0) & (z > 0)) | ((k == 1) & (z < PLANES - 1)) | (k == 2) | ((k == 3) & at_end)

            @pl.when(there)
            def _():
                copy = pltpu.make_async_copy(late_ref.at[k], late, sem)
                copy.start()
                copy.wait()
                plane = jnp.where(k == 0, z - 1, jnp.where(k == 1, z + 1, jnp.where(k == 2, z ^ 2, z ^ 3)))
                for half in range(2):
                    part = late.at[half * more : half * more + more, :]
                    unpack(t, tab, s_ref, lanes_ref, total, part, plane, half, cap)

            return carry

        lax.fori_loop(0, PLANE, step, 0)

    for k in range(width // lanes):
        out_ref[:, k * lanes : (k + 1) * lanes] = lanes_ref[k * total : (k + 1) * total, :]


def late_kernel(t, cap, tab, s_ref, values, message):
    rows = values.shape[2]
    to, flip = pl.program_id(0), pl.program_id(1)
    me = tab[t.me]
    block = jnp.where(
        to == 0,
        below(me, t.blocks),
        jnp.where(to == 1, above(me, t.blocks), jnp.where(to == 2, across(me, t.blocks), mirror(me, t.blocks))),
    )
    more = message.shape[1] // 2
    slot_ids = lax.broadcasted_iota(jnp.int32, (rows, more), 1) + cap
    hot = slots(tab, t, s_ref, me ^ flip, block, rows, s_ref.shape[2]) == slot_ids
    hi, lo = split(values[0, 0])
    part = dot_t(hot.astype(BF16), hi) + dot_t(hot.astype(BF16), lo)
    for half in range(2):
        at = slice(half * more, half * more + more)

        @pl.when(flip == 2 * half)
        def _(at=at):
            message[0, at, :] = part

        @pl.when(flip == 2 * half + 1)
        def _(at=at):
            message[0, at, :] += part


def vmem():
    return pl.BlockSpec(memory_space=pltpu.VMEM)


def smem():
    return pl.BlockSpec(memory_space=pltpu.SMEM)


def params(limit=VMEM_BYTES):
    return pltpu.CompilerParams(vmem_limit_bytes=limit)


def cost(flops, bytes_accessed):
    return pl.CostEstimate(
        flops=int(flops) // SCALE, bytes_accessed=int(bytes_accessed) // SCALE, transcendentals=0
    )


def after(x, *others):
    return lax.optimization_barrier((x, *others))[0]


def planes_body(cap, table, root_inverse, panels, diag_blocks, structure3):
    rows, total = root_inverse.shape
    children = structure3.shape[0]
    blocks = total // rows
    width = panels.shape[2]
    t = Table(children, blocks)

    def permute(x, move):
        return lax.ppermute(x, "row", [(r, move(r)) for r in range(blocks)])

    def along(x, planes, step):
        return lax.ppermute(
            x, "row", [(p * PLANE + b, (p + step) * PLANE + b) for p in planes for b in range(PLANE)]
        )

    def mirrored(x):
        ends = (0, PLANES - 1)
        return lax.ppermute(
            x, "row", [(p * PLANE + b, (PLANES - 1 - p) * PLANE + b) for p in ends for b in range(PLANE)]
        )

    def spread(flips, *given):
        unroll = 4
        shape = jax.ShapeDtypeStruct((len(flips), total, width), BF16)
        out = pl.BlockSpec((1, unroll * rows, width), lambda c, i: (c, i, 0))
        return pl.pallas_call(
            functools.partial(spread_kernel, t, flips, unroll),
            grid=(len(flips), blocks // unroll),
            out_shape=(shape, shape),
            in_specs=[smem(), vmem()] + [vmem()] * len(given),
            out_specs=(out, out),
            compiler_params=params(16 * MIB),
            cost_estimate=cost(8 * len(flips) * total * rows * 2 * width, 12 * len(flips) * total * width),
            name="spread",
        )(table, structure3, *given)

    def product(flips, here, deltas, factors, priors, given, summed=False, there=(), rest=None, panels=()):
        m = rows * len(given)
        message = jax.ShapeDtypeStruct((cap, width), F32)
        square = jax.ShapeDtypeStruct((width, width), F32)
        factor = jax.ShapeDtypeStruct((2, total, width), BF16)
        partial_sums = [square, square] if summed else []
        still = pl.BlockSpec((width, width), lambda c: (0, 0))
        whole = pl.BlockSpec((1, total, width), lambda c: (c, 0, 0))
        other_products = [rest] if there else []
        made = 2 if panels else 0
        return pl.pallas_call(
            functools.partial(
                product_kernel, t, flips, here, there, summed, bool(panels), deltas, cap, len(priors)
            ),
            grid=(2,),
            out_shape=[factor] * made
            + [jax.ShapeDtypeStruct((2, m, width), F32)]
            + partial_sums
            + [message] * len(deltas),
            in_specs=[smem(), vmem()]
            + [vmem()] * (len(priors) + len(given) + len(panels))
            + [pl.BlockSpec((1, rows * len(there), width), lambda c: (c, 0, 0))] * len(other_products)
            + [whole] * len(factors),
            out_specs=[whole] * made
            + [pl.BlockSpec((1, m, width), lambda c: (c, 0, 0))]
            + [still] * len(partial_sums)
            + [pl.BlockSpec((cap, width), lambda c: (0, 0))] * len(deltas),
            scratch_shapes=[pltpu.VMEM((2 * m, total), BF16)],
            compiler_params=params(28 * MIB),
            cost_estimate=cost(20 * m * total * width, 4 * len(given) * rows * total + 16 * total * width),
            name="product",
        )(table, structure3, *priors, *given, *panels, *other_products, *factors)

    def of_a(c):
        return jnp.minimum(c, 1)

    def of_b(c):
        return jnp.maximum(c - 2, 0)

    def final(factors_a, factors_b, third):
        a = pl.BlockSpec((1, total, width), lambda c: (of_a(c), 0, 0))
        b = pl.BlockSpec((1, total, width), lambda c: (of_b(c), 0, 0))
        return pl.pallas_call(
            functools.partial(last_kernel, t, cap),
            grid=(PLANE,),
            out_shape=(
                *[jax.ShapeDtypeStruct((1, rows, width), F32)] * PLANE,
                jax.ShapeDtypeStruct((2 * cap, width), F32),
            ),
            in_specs=[smem()] + [vmem()] * 2 + [a, a, b, b],
            out_specs=(
                *[pl.BlockSpec((1, rows, width), lambda c: (0, 0, 0))] * PLANE,
                pl.BlockSpec((2 * cap, width), lambda c: (0, 0)),
            ),
            scratch_shapes=[pltpu.VMEM((2 * rows, total), BF16)],
            compiler_params=params(20 * MIB),
            cost_estimate=cost(40 * rows * total * width, 32 * total * width),
            name="last",
        )(table, structure3, third, *factors_a, *factors_b)

    def finish(kept, sibling, other, last, others, factors):
        def factor(flip):
            return pl.BlockSpec(
                (1, rows, width), lambda i, tab: (0, mirror(tab[t.me] ^ flip, blocks), 0)
            )

        first_of = pl.BlockSpec((1, width, width), lambda i, tab: (0, 0, 0))
        pieces = [pl.BlockSpec((1, rows, width), lambda i, tab: (0, 0, 0))] * PLANE
        return pl.pallas_call(
            finish_kernel,
            out_shape=jax.ShapeDtypeStruct((1, width, width), F32),
            grid_spec=pltpu.PrefetchScalarGridSpec(
                num_scalar_prefetch=1,
                grid=(1,),
                in_specs=[first_of]
                + [pl.BlockSpec((width, width), lambda i, tab: (0, 0))] * 3
                + pieces
                + [factor(flip) for flip in range(PLANE)] * 2,
                out_specs=first_of,
            ),
            compiler_params=params(12 * MIB),
            cost_estimate=cost(12 * rows * width * width, 40 * rows * width + 20 * width * width),
            name="finish",
        )(table, diag_blocks, kept, sibling, other, last[0], *others, *([factors[0]] * PLANE), *([factors[1]] * PLANE))

    first, second = (0, 1), (2, 3)
    near_to = ((1, below), (2, above))
    panel_1 = permute(panels, lambda r: r ^ 1)
    panel_2 = permute(panels, lambda r: r ^ 2)
    from_below = along(root_inverse, range(PLANES - 1), 1)
    from_above = along(root_inverse, range(1, PLANES), -1)
    factors_a = spread(first, panels, panel_1)

    below_2 = along(after(from_below, *factors_a), range(1, PLANES - 1), 1)
    above_2 = along(after(from_above, *factors_a), range(1, PLANES - 1), -1)
    near, far = (own, below, above), (across,)
    nearby = (root_inverse, from_below, from_above)
    near_a, down_a, up_a = product(first, near, near_to, factors_a, (), nearby)
    across_2 = below_2 + above_2
    middle = range(PLANE, (PLANES - 1) * PLANE)
    mirror_3 = lax.ppermute(
        after(across_2, near_a), "row", [(r, r + PLANE if r >= 2 * PLANE else r - PLANE) for r in middle]
    )
    panel_3 = permute(after(panel_2, across_2, near_a), lambda r: r ^ 1)
    got_below_a = along(up_a, range(PLANES - 1), 1)
    got_above_a = along(down_a, range(1, PLANES), -1)
    far_a, kept_a, sent_a, twice_a = product(
        first, far, ((0, across),), factors_a, (), (across_2,), True, near, near_a
    )
    got_across_a = permute(twice_a, lambda r: r ^ (2 * PLANE))
    early = (got_below_a, got_above_a, got_across_a)
    nearby = (root_inverse, from_below, from_above, across_2)
    hi_b, lo_b, near_b, kept_b, sent_b, down, up, twice = product(
        second, near + far, near_to + ((3, across),), (), (), nearby, True,
        panels=(after(panel_2, kept_a), panel_3),
    )
    factors_b = (hi_b, lo_b)
    got_below = along(up, range(PLANES - 1), 1)
    got_above = along(down, range(1, PLANES), -1)
    got_across = permute(twice, lambda r: r ^ (2 * PLANE))
    sibling_a = permute(after(sent_a, mirror_3, *early), lambda r: r ^ 1)
    sibling_b = permute(after(sent_b, mirror_3, *early), lambda r: r ^ 1)
    other = permute(kept_b + sibling_b, lambda r: r ^ 2)
    *last, thrice = final(factors_a, factors_b, after(mirror_3, near_b))
    got_mirror = mirrored(after(thrice, got_across, got_below, got_above))
    others = [
        permute(last[flip], functools.partial(lambda flip, r: r ^ flip, flip))
        for flip in range(1, PLANE)
    ]
    child_inverse = finish(kept_a, sibling_a, other, last, others, factors_a)

    here = pl.BlockSpec((2, rows, width), lambda i: (0, 0, 0))
    flat = rows * children
    by_lanes = pl.pallas_call(
        functools.partial(unpack_kernel, t),
        grid=(1,),
        out_shape=jax.ShapeDtypeStruct((flat * (width // LANES), LANES), F32),
        in_specs=[smem(), vmem(), here, here] + [vmem()] * 6,
        out_specs=vmem(),
        compiler_params=params(16 * MIB),
        cost_estimate=cost(4 * flat * cap * width, 4 * (flat + 5 * cap) * width),
        name="unpack",
    )(table, structure3, near_a, near_b, *early, got_below, got_above, got_across)

    more = 2 * rows - cap

    def late(near_a, far_a, near_b, *last):
        to_below, to_above, to_across = (
            jnp.concatenate([near_a[:, k * rows : (k + 1) * rows] if k < 3 else far_a,
                             near_b[:, k * rows : (k + 1) * rows]])
            for k in (1, 2, 3)
        )
        values = jnp.stack([to_below, to_above, to_across, jnp.concatenate(last)])
        packed = pl.pallas_call(
            functools.partial(late_kernel, t, cap),
            grid=(PLANE, PLANE),
            out_shape=jax.ShapeDtypeStruct((PLANE, 2 * more, width), F32),
            in_specs=[smem(), vmem(), pl.BlockSpec((1, 1, rows, width), lambda k, c: (k, c, 0, 0))],
            out_specs=pl.BlockSpec((1, 2 * more, width), lambda k, c: (k, 0, 0)),
            compiler_params=params(16 * MIB),
            name="late",
        )(table, structure3, values)
        return jnp.stack(
            [
                along(packed[1], range(PLANES - 1), 1),
                along(packed[0], range(1, PLANES), -1),
                permute(packed[2], lambda r: r ^ (2 * PLANE)),
                mirrored(packed[3]),
            ]
        )

    def none(*unused):
        return jnp.zeros((PLANE, 2 * more, width), F32)

    beyond = lax.cond(table[t.over] != 0, late, none, after(near_a, got_mirror, child_inverse, by_lanes), far_a, near_b, *last)
    block_rows = pl.pallas_call(
        functools.partial(expand_kernel, t),
        out_shape=jax.ShapeDtypeStruct((flat, width), F32),
        in_specs=[smem()] + [vmem()] * 2 + [pl.BlockSpec(memory_space=pl.ANY)] * 2,
        out_specs=vmem(),
        scratch_shapes=[
            pltpu.VMEM((2 * more, width), F32),
            pltpu.VMEM((flat * (width // LANES), LANES), F32),
            pltpu.SemaphoreType.DMA,
        ],
        compiler_params=params(16 * MIB),
        cost_estimate=cost(flat * cap * width, 8 * flat * width),
        name="expand",
    )(table, structure3, got_mirror, after(by_lanes, child_inverse), beyond)
    return block_rows.reshape(rows, children, width), child_inverse


def planes(root_inverse, panels, diag_blocks, structure, live):
    rows, total = root_inverse.shape
    children, padded = structure.shape
    blocks = total // rows
    positions = jnp.arange(padded, dtype=jnp.int32)
    block_of = jnp.where(positions[None, :] < live[:, None], structure // rows, blocks)
    edges = jnp.arange(blocks + 1, dtype=jnp.int32)
    first = jnp.sum((block_of[:, None, :] < edges[None, :, None]).astype(jnp.int32), axis=2)
    counts = (first[:, 1:] - first[:, :-1]).reshape(children // 2, 2, blocks)
    largest = jnp.max(counts[:, 0] + counts[:, 1])
    offset = jnp.stack([jnp.zeros_like(counts[:, 0]), counts[:, 0]], axis=1).reshape(children, blocks)
    cap = rows + rows // 8
    table = jnp.concatenate(
        [
            first[:, :-1].reshape(-1),
            offset.reshape(-1),
            live,
            lax.axis_index("row").astype(jnp.int32)[None],
            (largest > cap).astype(jnp.int32)[None],
        ]
    )
    return planes_body(
        cap, table, root_inverse, panels, diag_blocks, structure.reshape(children, 1, padded)
    )


def body(root_inverse, panels, diag_blocks, structure, live):
    me = lax.axis_index("row")
    rows_here = root_inverse.shape[0]
    padded = structure.shape[1]
    width = panels.shape[2]
    total_rows = rows_here * lax.axis_size("row")
    mine = lax.dynamic_index_in_dim(structure, me, 0, keepdims=False)
    count = lax.dynamic_index_in_dim(live, me, 0, keepdims=False)
    columns = jnp.take(lax.all_gather(root_inverse, "row", axis=0, tiled=True), mine, axis=1)
    sub = jnp.take(columns, mine, axis=0)
    positions = jnp.arange(padded, dtype=jnp.int32)
    mask = (positions < count).astype(jnp.float32)
    masked = panels[0] * mask[:, None]
    off = -jnp.dot(sub, masked, precision=lax.Precision.HIGHEST) * mask[:, None]
    inner = diag_blocks[0] - jnp.dot(masked.T, off, precision=lax.Precision.HIGHEST)
    spread = jnp.zeros((total_rows, width), jnp.float32).at[mine].add(off)
    block_rows = lax.all_to_all(
        spread.reshape(total_rows, 1, width), "row", split_axis=0, concat_axis=1, tiled=True
    )
    return (block_rows, inner[None])


def solution(mesh):
    placed = (
        P(("pole", "row"), None),
        P(("pole", "row"), None, None),
        P(("pole", "row"), None, None),
        P(),
        P(),
    )
    return jax.shard_map(
        planes if mesh.shape["row"] == PLANES * PLANE else body,
        mesh=mesh,
        in_specs=placed,
        out_specs=(P(("pole", "row"), None, None), P(("pole", "row"), None, None)),
        check_vma=False,
    )
```

```python
import functools

import jax
import jax.numpy as jnp
from jax import lax
from jax.experimental import pallas as pl
from jax.experimental.pallas import tpu as pltpu
from jax.sharding import PartitionSpec as P

F32 = jnp.float32
BF16 = jnp.bfloat16
PLANES = 4
PLANE = 4
LANES = 128
SCALE = 16
VMEM_BYTES = 36 * 1024 * 1024
MIB = 1024 * 1024


def split(x):
    hi = x.astype(BF16)
    return hi, (x - hi.astype(F32)).astype(BF16)


def dot(a, b):
    return jnp.dot(a, b, preferred_element_type=F32)


def dot_t(a, b):
    return lax.dot_general(a, b, (((0,), (0,)), ((), ())), preferred_element_type=F32)


class Table:
    def __init__(self, children, blocks):
        self.children, self.blocks = children, blocks
        self.first = 0
        self.offset = children * blocks
        self.live = 2 * children * blocks
        self.me = self.live + children
        self.over = self.me + 1


def window(tab, t, s_ref, child, block, rows, padded):
    span = min(2 * rows, padded)
    begin = tab[t.first + child * t.blocks + block]
    at = pl.multiple_of(jnp.minimum((begin // rows) * rows, padded - span), rows)
    row_ids = lax.broadcasted_iota(jnp.int32, (rows, span), 0) + block * rows
    positions = lax.broadcasted_iota(jnp.int32, (rows, span), 1) + at
    hit = (row_ids == s_ref[child, :, pl.ds(at, span)]) & (positions < tab[t.live + child])
    return at, span, positions, hit


def slots(tab, t, s_ref, child, block, rows, padded):
    _, _, positions, hit = window(tab, t, s_ref, child, block, rows, padded)
    shift = tab[t.offset + child * t.blocks + block] - tab[t.first + child * t.blocks + block]
    return jnp.max(jnp.where(hit, positions + shift, -1), axis=1, keepdims=True)


def spread_block(t, tab, s_ref, child, block, rows, panel, hi_ref, lo_ref, to):
    at, span, _, hit = window(tab, t, s_ref, child, block, rows, s_ref.shape[2])
    hot = hit.astype(BF16)
    hi, lo = split(panel[0, pl.ds(at, span), :])
    hi_ref[0, to, :] = dot(hot, hi).astype(BF16)
    lo_ref[0, to, :] = dot(hot, lo).astype(BF16)


def spread_kernel(t, flips, unroll, tab, s_ref, *refs):
    panels, (hi_ref, lo_ref) = refs[: len(flips)], refs[len(flips) :]
    rows = hi_ref.shape[1] // unroll
    for c, flip in enumerate(flips):

        @pl.when(pl.program_id(0) == c)
        def _():
            child = tab[t.me] ^ flip
            for u in range(unroll):
                block = pl.program_id(1) * unroll + u
                to = slice(u * rows, (u + 1) * rows)
                spread_block(t, tab, s_ref, child, block, rows, panels[c], hi_ref, lo_ref, to)


def product_kernel(t, flips, here, there, summed, spreads, deltas, cap, prior, tab, s_ref, *refs):
    count = len(here)
    priors, blocks, refs = refs[:prior], refs[prior : prior + count], refs[prior + count :]
    if spreads:
        panels, refs = refs[:2], refs[2:]
    if there:
        before, refs = refs[:2], refs[2:]
    hi_ref, lo_ref, out_ref, refs = refs[0], refs[1], refs[2], refs[3:]
    if summed:
        kept_ref, sent_ref, refs = refs[0], refs[1], refs[2:]
    messages, x_ref = refs[:-1], refs[-1]
    rows = blocks[0].shape[0]
    m = rows * count
    padded = s_ref.shape[2]
    me = tab[t.me]
    step = pl.program_id(0)

    @pl.when(step == 0)
    def _():
        for k in range(count):
            hi, lo = split(blocks[k][...])
            x_ref[pl.ds(k * rows, rows), :] = hi
            x_ref[pl.ds(m + k * rows, rows), :] = lo

    if spreads:
        for c, flip in enumerate(flips):

            @pl.when(step == c)
            def _(panel=panels[c], flip=flip):
                for block in range(t.blocks):
                    to = slice(block * rows, (block + 1) * rows)
                    spread_block(t, tab, s_ref, me ^ flip, block, rows, panel, hi_ref, lo_ref, to)

    both = dot(x_ref[...], hi_ref[0])
    product = both[:m] + both[m:] + dot(x_ref[:m, :], lo_ref[0])
    out_ref[0] = product
    child = me ^ jnp.where(step == 0, flips[0], flips[1])
    slot_ids = lax.broadcasted_iota(jnp.int32, (rows, cap), 1)
    for n, (message, (k, delta)) in enumerate(zip(messages, deltas)):
        hot = slots(tab, t, s_ref, child, delta(me, t.blocks), rows, padded) == slot_ids
        hi, lo = split(product[k * rows : (k + 1) * rows])
        part = dot_t(hot.astype(BF16), hi) + dot_t(hot.astype(BF16), lo)

        @pl.when(step == 0)
        def _(n=n, message=message, part=part):
            message[...] = part + priors[n][...] if prior else part

        @pl.when(step != 0)
        def _(message=message, part=part):
            message[...] += part

    if summed:
        at = [pl.multiple_of(delta(me, t.blocks) * rows, rows) for delta in here]
        bh = jnp.concatenate([hi_ref[0, pl.ds(k, rows), :] for k in at], axis=0)
        bl = jnp.concatenate([lo_ref[0, pl.ds(k, rows), :] for k in at], axis=0)
        hi, lo = split(product)
        inner = dot_t(bh, hi) + dot_t(bh, lo) + dot_t(bl, hi)

        @pl.when(step == 0)
        def _():
            kept_ref[...] = inner + before[0][...] if there else inner

        @pl.when(step != 0)
        def _():
            sent_ref[...] = inner + before[1][...] if there else inner


def last_kernel(t, cap, tab, s_ref, third_ref, hi_a, lo_a, hi_b, lo_b, *refs):
    outs, (message, x_ref) = refs[:PLANE], refs[PLANE:]
    rows = third_ref.shape[0]
    padded = s_ref.shape[2]
    me = tab[t.me]
    step = pl.program_id(0)

    @pl.when(step == 0)
    def _():
        hi, lo = split(third_ref[...])
        x_ref[:rows, :] = hi
        x_ref[rows:, :] = lo

    slot_ids = lax.broadcasted_iota(jnp.int32, (rows, cap), 1)
    for flip, (hi_ref, lo_ref) in enumerate(((hi_a, lo_a), (hi_a, lo_a), (hi_b, lo_b), (hi_b, lo_b))):

        @pl.when(step == flip)
        def _(flip=flip, hi_ref=hi_ref, lo_ref=lo_ref):
            both = dot(x_ref[...], hi_ref[0])
            product = both[:rows] + both[rows:] + dot(x_ref[:rows, :], lo_ref[0])
            outs[flip][0] = product
            hot = slots(tab, t, s_ref, me ^ flip, mirror(me, t.blocks), rows, padded) == slot_ids
            hi, lo = split(product)
            part = dot_t(hot.astype(BF16), hi) + dot_t(hot.astype(BF16), lo)
            to = slice(flip // 2 * cap, flip // 2 * cap + cap)
            if flip % 2 == 0:
                message[to, :] = part
            else:
                message[to, :] += part


def finish_kernel(tab, diag_ref, kept_ref, sibling_ref, other_ref, *refs):
    products, (factors_hi, factors_lo, out_ref) = refs[:4], (refs[4:8], refs[8:12], refs[12])
    hi, lo = split(jnp.concatenate([g[0] for g in products], axis=0))
    bh = jnp.concatenate([b[0] for b in factors_hi], axis=0)
    bl = jnp.concatenate([b[0] for b in factors_lo], axis=0)
    added = dot_t(bh, hi) + dot_t(bh, lo) + dot_t(bl, hi)
    out_ref[0] = diag_ref[0] + (kept_ref[...] + sibling_ref[...] + other_ref[...] + added)


def own(me, blocks):
    return me


def below(me, blocks):
    return jnp.maximum(me - PLANE, 0)


def above(me, blocks):
    return jnp.minimum(me + PLANE, blocks - 1)


def across(me, blocks):
    return me ^ (2 * PLANE)


def mirror(me, blocks):
    return me ^ (3 * PLANE)


def store(lanes_ref, t, total, width, child, value, late=0):
    lanes = lanes_ref.shape[1]
    for k in range(width // lanes):
        to = pl.ds(k * total + child, total // t.children, stride=t.children)
        part = value[:, k * lanes : (k + 1) * lanes]
        lanes_ref[to, :] = lanes_ref[to, :] + part if late else part


def unpack(t, tab, s_ref, lanes_ref, total, message, plane, half, late=0):
    cap, width = message.shape
    rows = total // t.children
    me = tab[t.me]
    slot_ids = lax.broadcasted_iota(jnp.int32, (rows, cap), 1) + late
    hi, lo = split(message[...])
    first = plane * PLANE + ((me % PLANE) ^ (2 * half)) // 2 * 2
    for c in range(2):
        hot = slots(tab, t, s_ref, first + c, me, rows, s_ref.shape[2]) == slot_ids
        hot = hot.astype(BF16)
        store(lanes_ref, t, total, width, first + c, -(dot(hot, hi) + dot(hot, lo)), late)


def unpack_kernel(t, tab, s_ref, near_a, near_b, *refs):
    messages, (target, lanes_ref, sem) = refs[:-3], refs[-3:]
    rows, width = near_a.shape[1:]
    total = rows * t.children
    me = tab[t.me]
    z = me // PLANE
    for flip in range(PLANE):
        child = me ^ flip
        here = slots(tab, t, s_ref, child, me, rows, s_ref.shape[2]) >= 0
        value = (near_a, near_b)[flip // 2][flip % 2]
        store(lanes_ref, t, total, width, child, jnp.where(here, -value, 0.0))
    for half in range(2):
        below_ref, above_ref, across_ref = messages[3 * half : 3 * half + 3]

        @pl.when(z > 0)
        def _(below_ref=below_ref, half=half):
            unpack(t, tab, s_ref, lanes_ref, total, below_ref, z - 1, half)

        @pl.when(z < PLANES - 1)
        def _(above_ref=above_ref, half=half):
            unpack(t, tab, s_ref, lanes_ref, total, above_ref, z + 1, half)

        unpack(t, tab, s_ref, lanes_ref, total, across_ref, z ^ 2, half)

    copy = pltpu.make_async_copy(lanes_ref, target, sem)
    copy.start()
    copy.wait()


def expand_kernel(t, tab, s_ref, message, lanes_in, late_ref, out_ref, late, lanes_ref, sem, sems):
    total, width = out_ref.shape
    lanes = lanes_ref.shape[1]
    cap, more = message.shape[0] // 2, late.shape[0] // 2
    z = tab[t.me] // PLANE
    at_end = (z == 0) | (z == PLANES - 1)
    whole = pltpu.make_async_copy(lanes_in, lanes_ref, sem)
    whole.start()
    whole.wait()

    @pl.when(at_end)
    def _():
        for half in range(2):
            part = message.at[half * cap : half * cap + cap, :]
            unpack(t, tab, s_ref, lanes_ref, total, part, z ^ 3, half)

    @pl.when(tab[t.over] != 0)
    def _():
        def step(k, carry):
            there = ((k == 0) & (z > 0)) | ((k == 1) & (z < PLANES - 1)) | (k == 2) | ((k == 3) & at_end)

            @pl.when(there)
            def _():
                copy = pltpu.make_async_copy(late_ref.at[k], late, sem)
                copy.start()
                copy.wait()
                plane = jnp.where(k == 0, z - 1, jnp.where(k == 1, z + 1, jnp.where(k == 2, z ^ 2, z ^ 3)))
                for half in range(2):
                    part = late.at[half * more : half * more + more, :]
                    unpack(t, tab, s_ref, lanes_ref, total, part, plane, half, cap)

            return carry

        lax.fori_loop(0, PLANE, step, 0)

    copies = [
        pltpu.make_async_copy(
            lanes_ref.at[k * total : (k + 1) * total, :],
            out_ref.at[:, k * lanes : (k + 1) * lanes],
            sems.at[k],
        )
        for k in range(width // lanes)
    ]
    for copy in copies:
        copy.start()
    for copy in copies:
        copy.wait()


def late_kernel(t, cap, tab, s_ref, values, message):
    rows = values.shape[2]
    to, flip = pl.program_id(0), pl.program_id(1)
    me = tab[t.me]
    block = jnp.where(
        to == 0,
        below(me, t.blocks),
        jnp.where(to == 1, above(me, t.blocks), jnp.where(to == 2, across(me, t.blocks), mirror(me, t.blocks))),
    )
    more = message.shape[1] // 2
    slot_ids = lax.broadcasted_iota(jnp.int32, (rows, more), 1) + cap
    hot = slots(tab, t, s_ref, me ^ flip, block, rows, s_ref.shape[2]) == slot_ids
    hi, lo = split(values[0, 0])
    part = dot_t(hot.astype(BF16), hi) + dot_t(hot.astype(BF16), lo)
    for half in range(2):
        at = slice(half * more, half * more + more)

        @pl.when(flip == 2 * half)
        def _(at=at):
            message[0, at, :] = part

        @pl.when(flip == 2 * half + 1)
        def _(at=at):
            message[0, at, :] += part


def vmem():
    return pl.BlockSpec(memory_space=pltpu.VMEM)


def hbm():
    return pl.BlockSpec(memory_space=pltpu.HBM)


def smem():
    return pl.BlockSpec(memory_space=pltpu.SMEM)


def params(limit=VMEM_BYTES):
    return pltpu.CompilerParams(vmem_limit_bytes=limit)


def cost(flops, bytes_accessed):
    return pl.CostEstimate(
        flops=int(flops) // SCALE, bytes_accessed=int(bytes_accessed) // SCALE, transcendentals=0
    )


def after(x, *others):
    return lax.optimization_barrier((x, *others))[0]


def planes_body(cap, table, root_inverse, panels, diag_blocks, structure3):
    rows, total = root_inverse.shape
    children = structure3.shape[0]
    blocks = total // rows
    width = panels.shape[2]
    t = Table(children, blocks)

    def permute(x, move):
        return lax.ppermute(x, "row", [(r, move(r)) for r in range(blocks)])

    def along(x, planes, step):
        return lax.ppermute(
            x, "row", [(p * PLANE + b, (p + step) * PLANE + b) for p in planes for b in range(PLANE)]
        )

    def mirrored(x):
        ends = (0, PLANES - 1)
        return lax.ppermute(
            x, "row", [(p * PLANE + b, (PLANES - 1 - p) * PLANE + b) for p in ends for b in range(PLANE)]
        )

    def spread(flips, *given):
        unroll = 4
        shape = jax.ShapeDtypeStruct((len(flips), total, width), BF16)
        out = pl.BlockSpec((1, unroll * rows, width), lambda c, i: (c, i, 0))
        return pl.pallas_call(
            functools.partial(spread_kernel, t, flips, unroll),
            grid=(len(flips), blocks // unroll),
            out_shape=(shape, shape),
            in_specs=[smem(), vmem()] + [vmem()] * len(given),
            out_specs=(out, out),
            compiler_params=params(16 * MIB),
            cost_estimate=cost(8 * len(flips) * total * rows * 2 * width, 12 * len(flips) * total * width),
            name="spread",
        )(table, structure3, *given)

    def product(flips, here, deltas, factors, priors, given, summed=False, before=(), panels=()):
        m = rows * len(given)
        message = jax.ShapeDtypeStruct((cap, width), F32)
        square = jax.ShapeDtypeStruct((width, width), F32)
        factor = jax.ShapeDtypeStruct((2, total, width), BF16)
        partial_sums = [square, square] if summed else []
        still = pl.BlockSpec((width, width), lambda c: (0, 0))
        whole = pl.BlockSpec((1, total, width), lambda c: (c, 0, 0))
        other_sums = list(before)
        made = 2 if panels else 0
        return pl.pallas_call(
            functools.partial(
                product_kernel, t, flips, here, bool(before), summed, bool(panels), deltas, cap, len(priors)
            ),
            grid=(2,),
            out_shape=[factor] * made
            + [jax.ShapeDtypeStruct((2, m, width), F32)]
            + partial_sums
            + [message] * len(deltas),
            in_specs=[smem(), vmem()]
            + [vmem()] * (len(priors) + len(given) + len(panels))
            + [vmem()] * len(other_sums)
            + [whole] * len(factors),
            out_specs=[whole] * made
            + [pl.BlockSpec((1, m, width), lambda c: (c, 0, 0))]
            + [still] * len(partial_sums)
            + [pl.BlockSpec((cap, width), lambda c: (0, 0))] * len(deltas),
            scratch_shapes=[pltpu.VMEM((2 * m, total), BF16)],
            compiler_params=params(28 * MIB),
            cost_estimate=cost(20 * m * total * width, 4 * len(given) * rows * total + 16 * total * width),
            name="product",
        )(table, structure3, *priors, *given, *panels, *other_sums, *factors)

    def of_a(c):
        return jnp.minimum(c, 1)

    def of_b(c):
        return jnp.maximum(c - 2, 0)

    def final(factors_a, factors_b, third):
        a = pl.BlockSpec((1, total, width), lambda c: (of_a(c), 0, 0))
        b = pl.BlockSpec((1, total, width), lambda c: (of_b(c), 0, 0))
        return pl.pallas_call(
            functools.partial(last_kernel, t, cap),
            grid=(PLANE,),
            out_shape=(
                *[jax.ShapeDtypeStruct((1, rows, width), F32)] * PLANE,
                jax.ShapeDtypeStruct((2 * cap, width), F32),
            ),
            in_specs=[smem()] + [vmem()] * 2 + [a, a, b, b],
            out_specs=(
                *[pl.BlockSpec((1, rows, width), lambda c: (0, 0, 0))] * PLANE,
                pl.BlockSpec((2 * cap, width), lambda c: (0, 0)),
            ),
            scratch_shapes=[pltpu.VMEM((2 * rows, total), BF16)],
            compiler_params=params(20 * MIB),
            cost_estimate=cost(40 * rows * total * width, 32 * total * width),
            name="last",
        )(table, structure3, third, *factors_a, *factors_b)

    def finish(kept, sibling, other, last, others, factors):
        def factor(flip):
            return pl.BlockSpec(
                (1, rows, width), lambda i, tab: (0, mirror(tab[t.me] ^ flip, blocks), 0)
            )

        first_of = pl.BlockSpec((1, width, width), lambda i, tab: (0, 0, 0))
        pieces = [pl.BlockSpec((1, rows, width), lambda i, tab: (0, 0, 0))] * PLANE
        return pl.pallas_call(
            finish_kernel,
            out_shape=jax.ShapeDtypeStruct((1, width, width), F32),
            grid_spec=pltpu.PrefetchScalarGridSpec(
                num_scalar_prefetch=1,
                grid=(1,),
                in_specs=[first_of]
                + [pl.BlockSpec((width, width), lambda i, tab: (0, 0))] * 3
                + pieces
                + [factor(flip) for flip in range(PLANE)] * 2,
                out_specs=first_of,
            ),
            compiler_params=params(12 * MIB),
            cost_estimate=cost(12 * rows * width * width, 40 * rows * width + 20 * width * width),
            name="finish",
        )(table, diag_blocks, kept, sibling, other, last[0], *others, *([factors[0]] * PLANE), *([factors[1]] * PLANE))

    first, second = (0, 1), (2, 3)
    near_to = ((1, below), (2, above))
    panel_1 = permute(panels, lambda r: r ^ 1)
    panel_2 = permute(panels, lambda r: r ^ 2)
    from_below = along(root_inverse, range(PLANES - 1), 1)
    from_above = along(root_inverse, range(1, PLANES), -1)
    factors_a = spread(first, panels, panel_1)

    below_2 = along(after(from_below, *factors_a), range(1, PLANES - 1), 1)
    above_2 = along(after(from_above, *factors_a), range(1, PLANES - 1), -1)
    near, far = (own, below, above), (across,)
    nearby = (root_inverse, from_below, from_above)
    near_a, *sums_a, down_a, up_a = product(first, near, near_to, factors_a, (), nearby, True)
    across_2 = below_2 + above_2
    middle = range(PLANE, (PLANES - 1) * PLANE)
    mirror_3 = lax.ppermute(
        after(across_2, near_a), "row", [(r, r + PLANE if r >= 2 * PLANE else r - PLANE) for r in middle]
    )
    panel_3 = permute(after(panel_2, across_2, near_a), lambda r: r ^ 1)
    got_below_a = along(up_a, range(PLANES - 1), 1)
    got_above_a = along(down_a, range(1, PLANES), -1)
    far_a, kept_a, sent_a, twice_a = product(
        first, far, ((0, across),), factors_a, (), (across_2,), True, sums_a
    )
    got_across_a = permute(twice_a, lambda r: r ^ (2 * PLANE))
    early = (got_below_a, got_above_a, got_across_a)
    nearby = (root_inverse, from_below, from_above, across_2)
    hi_b, lo_b, near_b, kept_b, sent_b, down, up, twice = product(
        second, near + far, near_to + ((3, across),), (), (), nearby, True,
        panels=(after(panel_2, kept_a), panel_3),
    )
    factors_b = (hi_b, lo_b)
    got_below = along(up, range(PLANES - 1), 1)
    got_above = along(down, range(1, PLANES), -1)
    got_across = permute(twice, lambda r: r ^ (2 * PLANE))
    sibling_a = permute(after(sent_a, mirror_3, *early), lambda r: r ^ 1)
    sibling_b = permute(after(sent_b, mirror_3, *early), lambda r: r ^ 1)
    other = permute(kept_b + sibling_b, lambda r: r ^ 2)
    *last, thrice = final(factors_a, factors_b, after(mirror_3, near_b))
    got_mirror = mirrored(after(thrice, got_across, got_below, got_above))
    others = [
        permute(last[flip], functools.partial(lambda flip, r: r ^ flip, flip))
        for flip in range(1, PLANE)
    ]
    child_inverse = finish(kept_a, sibling_a, other, last, others, factors_a)

    here = pl.BlockSpec((2, rows, width), lambda i: (0, 0, 0))
    flat = rows * children
    by_lanes = pl.pallas_call(
        functools.partial(unpack_kernel, t),
        grid=(1,),
        out_shape=jax.ShapeDtypeStruct((flat * (width // LANES), LANES), F32),
        in_specs=[smem(), vmem(), here, here] + [vmem()] * 6,
        out_specs=hbm(),
        scratch_shapes=[pltpu.VMEM((flat * (width // LANES), LANES), F32), pltpu.SemaphoreType.DMA],
        compiler_params=params(16 * MIB),
        cost_estimate=cost(4 * flat * cap * width, 4 * (flat + 5 * cap) * width),
        name="unpack",
    )(table, structure3, near_a, near_b, *early, got_below, got_above, got_across)

    more = 2 * rows - cap

    def late(near_a, far_a, near_b, *last):
        to_below, to_above, to_across = (
            jnp.concatenate([near_a[:, k * rows : (k + 1) * rows] if k < 3 else far_a,
                             near_b[:, k * rows : (k + 1) * rows]])
            for k in (1, 2, 3)
        )
        values = jnp.stack([to_below, to_above, to_across, jnp.concatenate(last)])
        packed = pl.pallas_call(
            functools.partial(late_kernel, t, cap),
            grid=(PLANE, PLANE),
            out_shape=jax.ShapeDtypeStruct((PLANE, 2 * more, width), F32),
            in_specs=[smem(), vmem(), pl.BlockSpec((1, 1, rows, width), lambda k, c: (k, c, 0, 0))],
            out_specs=pl.BlockSpec((1, 2 * more, width), lambda k, c: (k, 0, 0)),
            compiler_params=params(16 * MIB),
            name="late",
        )(table, structure3, values)
        return jnp.stack(
            [
                along(packed[1], range(PLANES - 1), 1),
                along(packed[0], range(1, PLANES), -1),
                permute(packed[2], lambda r: r ^ (2 * PLANE)),
                mirrored(packed[3]),
            ]
        )

    def none(*unused):
        return jnp.zeros((PLANE, 2 * more, width), F32)

    beyond = lax.cond(table[t.over] != 0, late, none, after(near_a, got_mirror, child_inverse, by_lanes), far_a, near_b, *last)
    block_rows = pl.pallas_call(
        functools.partial(expand_kernel, t),
        out_shape=jax.ShapeDtypeStruct((flat, width), F32),
        in_specs=[smem()] + [vmem()] * 2 + [hbm()] * 2,
        out_specs=hbm(),
        scratch_shapes=[
            pltpu.VMEM((2 * more, width), F32),
            pltpu.VMEM((flat * (width // LANES), LANES), F32),
            pltpu.SemaphoreType.DMA,
            pltpu.SemaphoreType.DMA((width // LANES,)),
        ],
        compiler_params=params(16 * MIB),
        cost_estimate=cost(flat * cap * width, 8 * flat * width),
        name="expand",
    )(table, structure3, got_mirror, after(by_lanes, child_inverse), beyond)
    return block_rows.reshape(rows, children, width), child_inverse


def planes(root_inverse, panels, diag_blocks, structure, live):
    rows, total = root_inverse.shape
    children, padded = structure.shape
    blocks = total // rows
    positions = jnp.arange(padded, dtype=jnp.int32)
    block_of = jnp.where(positions[None, :] < live[:, None], structure // rows, blocks)
    edges = jnp.arange(blocks + 1, dtype=jnp.int32)
    first = jnp.sum((block_of[:, None, :] < edges[None, :, None]).astype(jnp.int32), axis=2)
    counts = (first[:, 1:] - first[:, :-1]).reshape(children // 2, 2, blocks)
    largest = jnp.max(counts[:, 0] + counts[:, 1])
    offset = jnp.stack([jnp.zeros_like(counts[:, 0]), counts[:, 0]], axis=1).reshape(children, blocks)
    cap = rows + rows // 8
    table = jnp.concatenate(
        [
            first[:, :-1].reshape(-1),
            offset.reshape(-1),
            live,
            lax.axis_index("row").astype(jnp.int32)[None],
            (largest > cap).astype(jnp.int32)[None],
        ]
    )
    return planes_body(
        cap, table, root_inverse, panels, diag_blocks, structure.reshape(children, 1, padded)
    )


def body(root_inverse, panels, diag_blocks, structure, live):
    me = lax.axis_index("row")
    rows_here = root_inverse.shape[0]
    padded = structure.shape[1]
    width = panels.shape[2]
    total_rows = rows_here * lax.axis_size("row")
    mine = lax.dynamic_index_in_dim(structure, me, 0, keepdims=False)
    count = lax.dynamic_index_in_dim(live, me, 0, keepdims=False)
    columns = jnp.take(lax.all_gather(root_inverse, "row", axis=0, tiled=True), mine, axis=1)
    sub = jnp.take(columns, mine, axis=0)
    positions = jnp.arange(padded, dtype=jnp.int32)
    mask = (positions < count).astype(jnp.float32)
    masked = panels[0] * mask[:, None]
    off = -jnp.dot(sub, masked, precision=lax.Precision.HIGHEST) * mask[:, None]
    inner = diag_blocks[0] - jnp.dot(masked.T, off, precision=lax.Precision.HIGHEST)
    spread = jnp.zeros((total_rows, width), jnp.float32).at[mine].add(off)
    block_rows = lax.all_to_all(
        spread.reshape(total_rows, 1, width), "row", split_axis=0, concat_axis=1, tiled=True
    )
    return (block_rows, inner[None])


def solution(mesh):
    placed = (
        P(("pole", "row"), None),
        P(("pole", "row"), None, None),
        P(("pole", "row"), None, None),
        P(),
        P(),
    )
    return jax.shard_map(
        planes if mesh.shape["row"] == PLANES * PLANE else body,
        mesh=mesh,
        in_specs=placed,
        out_specs=(P(("pole", "row"), None, None), P(("pole", "row"), None, None)),
        check_vma=False,
    )
```
